512 devices in a mesh: expert: 32 (over z, core), helper: 4 (over y), dp: 4 (over x).
Axes of the slice: x: 4, y: 4, z: 16, core: 2. Of those that a mesh axis runs over, the one named last changes fastest.
Arguments:
- inputs: bfloat16 [1536, 2880], P(('expert', 'dp')), may hold values from -6 to 6
- cotangent: bfloat16 [1536, 2880], P(('expert', 'dp')), may hold values from -6 to 6
- expert_ids: int32 [1536, 4], P(('expert', 'dp')), may hold values from 0 to 31, all different within a row; in each aligned block of 12 rows (0 to 11, 12 to 23, ...) at most 2 rows name the same one
- gate_values: float32 [1536, 4], P(('expert', 'dp')), may hold values from 0.1 to 1
- w_gate: bfloat16 [32, 2880, 2048], P('expert', None, ('helper', 'dp')), may hold values from -0.109375 to 0.109375
- w_up: bfloat16 [32, 2880, 2048], P('expert', None, ('helper', 'dp')), may hold values from -0.109375 to 0.109375
- w_down: bfloat16 [32, 2048, 2880], P('expert', ('helper', 'dp')), may hold values from -0.125 to 0.125
Outputs:
- grad_inputs: bfloat16 [1536, 2880], P(('expert', 'dp'), 'helper')
- grad_w_gate: bfloat16 [32, 2880, 2048], P('expert', None, ('helper', 'dp'))
- grad_w_up: bfloat16 [32, 2880, 2048], P('expert', None, ('helper', 'dp'))
- grad_w_down: bfloat16 [32, 2048, 2880], P('expert', ('helper', 'dp'))
The draws below stay inside these ranges and needn't reach their ends.
Inputs may be any that keep to these rules, and one draw needn't show every extreme that they name: `expert_ids`: each token names 4 different experts. Within each aligned block of 12 rows (the tokens of one token shard) no expert is named by more than 2 rows, a bound that some block reaches.
All inputs are finite; a program needn't handle non-finite values.
Results may differ from the reference program's by a relative error of at most 0.0064.
Values may be sent and summed in bfloat16 or wider, within the bound.
A program may use at most 128 MiB of HBM per device.

```python
import math
import jax
import jax.numpy as jnp
import numpy as np
from jax import lax

D = 2880
FF = 2048
E = 32
K = 4
TOK_DEV = 12
CAP = 2
TOKENS = 1536
N_HELPER = 4
N_DP = 4


def block_levels(own_key, dims, cuts, least, high):
    level = 1.0
    for axis_at, blocks in cuts:
        heights = jax.random.uniform(jax.random.fold_in(jax.random.fold_in(own_key, 6), axis_at), (blocks,), jnp.float32, least / len(cuts), high / len(cuts))
        level = level * jnp.repeat(jnp.exp(heights), dims[axis_at] // blocks).reshape((-1,) + (1,) * (len(dims) - 1 - axis_at))
    return level


def deal_out(rng, own, number, rows, number_of, top, most, skew):
    sequence = jax.random.permutation(rng, number_of)
    packed, common = load_shares(number_of, rows * top, most, skew, True), load_shares(number_of, rows * top, most, skew, False)
    places = jnp.arange(number_of)

    def named(sizes, rotation):
        used = int((sizes > 0).sum())
        fixed = max(1, used // 4)
        shifted = fixed + (places - fixed + rotation * (used - fixed)) % max(1, number_of - fixed)
        return jnp.zeros((number_of,), jnp.int32).at[sequence[jnp.where(places < fixed, places, shifted)]].set(jnp.asarray(sizes, jnp.int32))

    sizes = jnp.where(number % 4 == 0, named(packed, number // 4), named(common, number - number // 4 - 1))
    mixed = jax.random.permutation(jax.random.fold_in(own, 3), number_of)
    source_of, taker = mixed[0:number_of // 2 * 2:2], mixed[1:number_of // 2 * 2:2]
    room = jnp.minimum(sizes[source_of] - 1, most - sizes[taker]) // 2
    room = jnp.where((source_of == sequence[0]) | (taker == sequence[0]) | (sizes[taker] == 0), 0, jnp.maximum(room, 0))
    shifted = jax.random.randint(jax.random.fold_in(own, 4), (number_of // 2,), 0, 1 << 20) % (room + 1)
    sizes = sizes.at[source_of].add(-shifted).at[taker].add(shifted)
    members = jnp.searchsorted(jnp.cumsum(sizes), jnp.arange(rows * top), side="right").astype(jnp.int32)
    table = members.reshape(top, rows).T
    table = table[jax.random.permutation(jax.random.fold_in(own, 1), rows)]
    rotation = jax.random.randint(jax.random.fold_in(own, 2), (rows, 1), 0, top)
    return jnp.take_along_axis(table, (jnp.arange(top)[None, :] + rotation) % top, axis=1)


def load_shares(amount, total, most, skew, full):
    weights = [(1 << 20) // math.isqrt(standing ** skew) + 1 for standing in range(1, amount + 1)]
    largest = most if full else min(most, max(-(-total // amount), total * weights[0] // sum(weights)))
    least = 1 if total - largest >= amount - 1 else 0
    given, rest = [largest] + [least] * (amount - 1), total - largest - least * (amount - 1)
    while rest > 0:
        candidates = [i for i in range(1, amount) if given[i] < largest] or [i for i in range(1, amount) if given[i] < most]
        pool, budget = sum([weights[i] for i in candidates]), rest
        for i in candidates:
            extra = min(most - given[i], max(1, budget * weights[i] // pool), rest)
            given[i] = given[i] + extra
            rest = rest - extra
    return np.array(given)


def noise(key, extent, width, reach, cuts=(), held_as=jnp.bfloat16):
    result = jax.random.normal(key, extent, jnp.float32) * width
    if len(cuts) > 0:
        result = block_levels(key, extent, cuts, -0.22, 0.18) * result
    return jnp.clip(result, min=-reach, max=reach).astype(held_as)


def setup_inputs(seed: int = 0) -> dict:
    key_list = jax.random.split(jax.random.key(seed), 8)
    inputs = noise(key_list[0], (TOKENS, D), 1.0, 6.0, ((0, 128),))
    cotangent = noise(key_list[1], (TOKENS, D), 1.0, 6.0, ((0, 128),))
    expert_ids_keys = jax.random.split(jax.random.fold_in(key_list[2], 1), TOKENS // TOK_DEV)
    expert_ids_turns = jax.random.permutation(jax.random.fold_in(key_list[2], 3), TOKENS // TOK_DEV)
    expert_ids = jax.vmap(lambda own, number: deal_out(jax.random.fold_in(key_list[2], 2), own, number, TOK_DEV, E, K, CAP, 2))(expert_ids_keys, expert_ids_turns).reshape((TOKENS, K))
    gate_values = jnp.clip(0.1 + 0.9 * jax.random.uniform(key_list[3], (TOKENS, K), jnp.float32) ** block_levels(key_list[3], (TOKENS, K), ((0, 128),), -0.2, 0.2), 0.1, 1.0)
    w_gate = noise(key_list[4], (E, D, FF), D ** -0.5, 0.109375, ((0, 32), (2, 16)))
    w_up = noise(key_list[5], (E, D, FF), D ** -0.5, 0.109375, ((0, 32), (2, 16)))
    w_down = noise(key_list[6], (E, FF, D), FF ** -0.5, 0.125, ((0, 32), (1, 16)))
    return dict(inputs=inputs, cotangent=cotangent, expert_ids=expert_ids, gate_values=gate_values, w_gate=w_gate, w_up=w_up, w_down=w_down)


def reference(inputs, cotangent, expert_ids, gate_values, w_gate, w_up, w_down):
    tokens = inputs.shape[0]
    shards = tokens // TOK_DEV
    pairs = TOK_DEV * K
    shard_ids = expert_ids.reshape(shards, pairs)
    onehot = (shard_ids[:, :, None] == jnp.arange(E, dtype=jnp.int32)[None, None, :]).astype(jnp.int32)
    before = jnp.cumsum(onehot, axis=1) - onehot
    slot_index = shard_ids * CAP + lax.optimization_barrier(jnp.sum(before * onehot, axis=2))
    owner_row = jnp.arange(shards, dtype=jnp.int32)[:, None] * TOK_DEV + jnp.arange(pairs, dtype=jnp.int32)[None, :] // K
    shard_row = jnp.broadcast_to(jnp.arange(shards, dtype=jnp.int32)[:, None], (shards, pairs))
    table_tok = jnp.zeros((shards, E * CAP), jnp.int32).at[shard_row, slot_index].set(owner_row)
    table_gate = jnp.zeros((shards, E * CAP), jnp.float32).at[shard_row, slot_index].set(gate_values.reshape(shards, pairs))
    table_tok = table_tok.reshape(shards, E, CAP).transpose(1, 0, 2).reshape(E, shards * CAP)
    table_gate = table_gate.reshape(shards, E, CAP).transpose(1, 0, 2).reshape(E, shards * CAP)
    blocks = N_HELPER * N_DP
    width_block = FF // blocks

    def expert_grad(pieces):
        token_index, slot_gate, gate_w, up_w, down_w = pieces
        expert_rows = inputs[token_index]
        expert_cot = (slot_gate[:, None] * cotangent[token_index].astype(jnp.float32)).astype(jnp.bfloat16)
        gate_pre = jnp.dot(expert_rows, gate_w, preferred_element_type=jnp.float32)
        up_pre = jnp.dot(expert_rows, up_w, preferred_element_type=jnp.float32)
        sigmoid_gate = jax.nn.sigmoid(1.702 * gate_pre)
        activated = gate_pre * sigmoid_gate
        hidden = ((up_pre + 1.0) * activated).astype(jnp.bfloat16)
        d_hidden = jnp.dot(expert_cot, down_w.T, preferred_element_type=jnp.float32)
        d_up = (d_hidden * activated).astype(jnp.bfloat16)
        slope = sigmoid_gate + 1.702 * gate_pre * sigmoid_gate * (1.0 - sigmoid_gate)
        d_gate = (d_hidden * (up_pre + 1.0) * slope).astype(jnp.bfloat16)
        grad_down = jnp.dot(hidden.T, expert_cot, preferred_element_type=jnp.float32).astype(jnp.bfloat16)
        grad_up = jnp.dot(expert_rows.T, d_up, preferred_element_type=jnp.float32).astype(jnp.bfloat16)
        grad_gate = jnp.dot(expert_rows.T, d_gate, preferred_element_type=jnp.float32).astype(jnp.bfloat16)
        row_count = d_up.shape[0]
        partial_value = jnp.einsum('rbf,dbf->rbd', d_up.reshape(row_count, blocks, width_block).astype(jnp.float32), up_w.reshape(D, blocks, width_block).astype(jnp.float32))
        partial_value = partial_value + jnp.einsum('rbf,dbf->rbd', d_gate.reshape(row_count, blocks, width_block).astype(jnp.float32), gate_w.reshape(D, blocks, width_block).astype(jnp.float32))
        rounded = lax.optimization_barrier(partial_value.astype(jnp.bfloat16))
        return (lax.optimization_barrier(jnp.sum(rounded.astype(jnp.float32), axis=1)), grad_gate, grad_up, grad_down)
    partials, grad_gate, grad_up, grad_down = lax.map(expert_grad, (table_tok, table_gate, w_gate, w_up, w_down))
    grad_inputs = jnp.zeros((tokens, D), jnp.float32).at[table_tok.reshape(-1)].add(partials.reshape(-1, D))
    return (grad_inputs.astype(jnp.bfloat16), grad_gate, grad_up, grad_down)
```

```python
import functools

import jax
import jax.numpy as jnp
from jax import lax
from jax.experimental import pallas as pl
from jax.experimental.pallas import tpu as pltpu
from jax.sharding import PartitionSpec as P

CAP = 2
MESH = pl.DeviceIdType.MESH
F32 = jnp.float32
BF16 = jnp.bfloat16
NT = (((1,), (1,)), ((), ()))
TN = (((0,), (0,)), ((), ()))
NN = (((1,), (0,)), ((), ()))


def dot(a, b, dims=NN):
    return lax.dot_general(a, b, dims, preferred_element_type=F32)


def shift(i, y):
    return (1 + y, 8 - y, -y, y - 7)[i]


def pick_shift(i, y):
    return jnp.where(i == 0, 1 + y, jnp.where(i == 1, 8 - y, jnp.where(i == 2, -y, y - 7)))


def pick(idt, gvt, z, nz, i, y, core, j):
    far = z + pick_shift(i, y)
    far = jnp.where(far < 0, far + nz, jnp.where(far >= nz, far - nz, far))
    expert = far * 2 + core
    tokens = idt.shape[1]
    hits = [(idt[k : k + 1, :] == expert) for k in range(idt.shape[0])]
    named = functools.reduce(lambda a, b: a + b, [h.astype(F32) for h in hits])
    row = lax.broadcasted_iota(jnp.int32, (tokens, tokens), 0)
    col = lax.broadcasted_iota(jnp.int32, (tokens, tokens), 1)
    before = dot(named.astype(BF16), (row < col).astype(BF16))
    chosen = jnp.where(before == j.astype(F32), named, 0.0)
    weight = functools.reduce(lambda a, b: a + b, [h.astype(F32) * gvt[k : k + 1, :] for k, h in enumerate(hits)])
    return chosen, jnp.sum(chosen * weight, axis=1, keepdims=True)


def body(cuts, nz, x_ref, c_ref, idt_ref, gvt_ref, wg_hbm, wu_hbm, wd_hbm, gi_ref, gg_hbm, gu_hbm, gd_hbm, *rest):
    parts = len(cuts)
    sb, rb, gx, gc = (rest[n * parts : (n + 1) * parts] for n in range(4))
    (wcat, wd, gg, gu, gd, stage, pu, pv, ru, rv, qu, qv, su, sv, back, ts, tr,
     zs, zr, ags, agr, rss, rsr, ts_sem, tr_sem, wsem, osem) = rest[4 * parts :]
    e = lax.axis_index("expert")
    y = lax.axis_index("helper")
    x = lax.axis_index("dp")
    ne = 2 * nz
    z = e // 2
    c = e % 2
    model = x_ref.shape[1]
    quarter = model // 4

    loads = [
        pltpu.make_async_copy(wg_hbm, wcat.at[:, 0:128], wsem.at[0]),
        pltpu.make_async_copy(wu_hbm, wcat.at[:, 128:256], wsem.at[1]),
        pltpu.make_async_copy(wd_hbm, wd, wsem.at[2]),
    ]
    for load in loads:
        load.start()

    def ring(me):
        return (me + 1 + 2 * c) % 4, (me + 3 - 2 * c) % 4, (me + 2) % 4

    xa, xb, xo = ring(x)
    ya, yb, yo = ring(y)

    barrier = pltpu.get_barrier_semaphore()

    @pl.loop(1, ne)
    def _(n):
        pl.semaphore_signal(barrier, inc=1, device_id={"expert": (e + n) % ne}, device_id_type=MESH)

    for other in (xa, xb):
        pl.semaphore_signal(barrier, inc=1, device_id={"dp": other}, device_id_type=MESH)
    for other in (ya, yb):
        pl.semaphore_signal(barrier, inc=1, device_id={"helper": other}, device_id_type=MESH)

    idt = idt_ref[...]
    gvt = gvt_ref[...]
    r = lax.broadcasted_iota(jnp.int32, (32, 1), 0)
    half = (r // 2) % 2
    chosen, gate = pick(idt, gvt, z, nz, r // 8, y, (r // 4) % 2, r % 2)
    pick_x = jnp.where(half == 0, chosen, 0.0).astype(BF16)
    pick_c = jnp.where(half == 1, chosen, 0.0).astype(BF16)
    start = 0
    for h, width in enumerate(cuts):
        rows = dot(pick_x, x_ref[:, start : start + width]) + gate * dot(pick_c, c_ref[:, start : start + width])
        for s in range(8):
            sb[h][s] = rows[4 * s : 4 * s + 4, :].astype(BF16)
        start += width

    pl.semaphore_wait(barrier, ne - 1 + 4)

    for h in range(parts):
        for i in (1, 3, 0, 2):
            to = (z + shift(i, y) + nz) % nz
            for core in range(2):
                s = 2 * i + core
                far = pltpu.make_async_remote_copy(
                    sb[h].at[s], rb[h].at[2 * i + c], zs.at[h], zr.at[h],
                    device_id={"expert": to * 2 + core}, device_id_type=MESH,
                )
                if i == 2:
                    own = (y == 0) & (c == core)

                    @pl.when(own)
                    def _():
                        pltpu.make_async_copy(sb[h].at[s], rb[h].at[2 * i + c], zr.at[h]).start()

                    @pl.when(jnp.logical_not(own))
                    def _():
                        far.start()
                else:
                    far.start()

    def wait(ref, sem):
        pltpu.make_async_copy(ref, ref, sem).wait()

    class Gather:
        def __init__(self, view, me, axis, ends, h, a, phase):
            self.view, self.me, self.axis = view, me, axis
            self.ahead, self.behind, self.opposite = ends
            self.ss = [ags.at[h, a, phase, n] for n in range(3)]
            self.rs = [agr.at[h, a, phase, n] for n in range(3)]

        def copy(self, at, n, to):
            return pltpu.make_async_remote_copy(
                self.view(at), self.view(at), self.ss[n], self.rs[n],
                device_id={self.axis: to}, device_id_type=MESH,
            )

        def start(self):
            self.copy(self.me, 0, self.ahead).start()
            self.copy(self.me, 1, self.behind).start()

        def forward(self):
            wait(self.view(self.behind), self.rs[0])
            self.copy(self.behind, 2, self.ahead).start()

        def finish(self):
            wait(self.view(self.ahead), self.rs[1])
            wait(self.view(self.opposite), self.rs[2])

        def sent(self):
            wait(self.view(self.me), self.ss[0])
            wait(self.view(self.me), self.ss[1])
            wait(self.view(self.behind), self.ss[2])

    xends, yends = (xa, xb, xo), (ya, yb, yo)
    first = [
        (Gather(lambda n, h=h: gx[h].at[n, y], x, "dp", xends, h, 0, 0),
         Gather(lambda n, h=h: gc[h].at[x, n], y, "helper", yends, h, 1, 0))
        for h in range(parts)
    ]
    second = [
        (Gather(lambda n, h=h: gx[h].at[:, n], y, "helper", yends, h, 0, 1),
         Gather(lambda n, h=h: gc[h].at[n], x, "dp", xends, h, 1, 1))
        for h in range(parts)
    ]

    def arrive(h):
        wait(rb[h], zr.at[h])
        width = cuts[h]
        for s in range(8):
            rows = rb[h][s].astype(F32)
            stage[2 * s : 2 * s + 2, 0:width] = rows[0:2]
            stage[16 + 2 * s : 18 + 2 * s, 0:width] = rows[2:4]
        gx[h][x, y] = stage[0:16, 0:width].astype(BF16)
        gc[h][x, y] = stage[16:32, 0:width].astype(BF16)
        for g in first[h]:
            g.start()

    def run(group, what):
        for g in group:
            getattr(g, what)()

    for h in range(parts):
        arrive(h)
        run(first[h], "forward")
        if h:
            run(second[h - 1], "forward")
        run(first[h], "finish")
        run(second[h], "start")

    total = 256
    pre = jnp.zeros((total, 256), F32)
    d_hidden = jnp.zeros((total, 128), F32)
    start = 0
    for h in range(parts):
        if h == parts - 1:
            run(second[h], "forward")
        run(second[h], "finish")
        if h == 0:
            for load in loads:
                load.wait()
        width = cuts[h]
        pre = pre + dot(gx[h][...].reshape(total, width), wcat[start : start + width, :])
        d_hidden = d_hidden + dot(gc[h][...].reshape(total, width), wd[start : start + width, :])
        start += width

    gate_pre = pre[:, 0:128]
    up1 = pre[:, 128:256] + 1.0
    sig = jax.nn.sigmoid(1.702 * gate_pre)
    activated = gate_pre * sig
    hidden = (up1 * activated).astype(BF16)
    d_up = (d_hidden * activated).astype(BF16)
    d_gate = (d_hidden * up1 * (sig + 1.702 * gate_pre * sig * (1.0 - sig))).astype(BF16)
    dcat = jnp.concatenate([d_gate, d_up], axis=1)

    for q in range(4):
        part = dot(dcat, wcat[quarter * q : quarter * (q + 1), :], NT)
        for n in range(4):
            pu[n, q] = part[64 * n : 64 * n + 32, :].astype(BF16)
            pv[n, q] = part[64 * n + 32 : 64 * n + 64, :].astype(BF16)

    class Scatter:
        def __init__(self, view, land, me, axis, ends, a, phase):
            self.view, self.land, self.me, self.axis = view, land, me, axis
            self.ahead, self.behind, self.opposite = ends
            self.ss = [rss.at[a, phase, n] for n in range(3)]
            self.rs = [rsr.at[a, phase, n] for n in range(3)]

        def copy(self, at, n, to):
            return pltpu.make_async_remote_copy(
                self.view(at), self.land.at[n], self.ss[n], self.rs[n],
                device_id={self.axis: to}, device_id_type=MESH,
            )

        def start(self):
            self.copy(self.opposite, 0, self.ahead).start()
            self.copy(self.behind, 1, self.behind).start()

        def forward(self):
            wait(self.land.at[0], self.rs[0])
            ref = self.view(self.ahead)
            ref[...] = (ref[...].astype(F32) + self.land[0].astype(F32)).astype(BF16)
            self.copy(self.ahead, 2, self.ahead).start()

        def finish(self):
            wait(self.land.at[1], self.rs[1])
            wait(self.land.at[2], self.rs[2])
            return self.view(self.me)[...].astype(F32) + self.land[1].astype(F32) + self.land[2].astype(F32)

        def sent(self):
            for n in range(3):
                wait(self.land.at[n], self.ss[n])

    u1 = Scatter(lambda n: pu.at[n], ru, x, "dp", xends, 0, 0)
    v1 = Scatter(lambda n: pv.at[:, n], rv, y, "helper", yends, 1, 0)
    u2 = Scatter(lambda n: qu.at[n], su, y, "helper", yends, 0, 1)
    v2 = Scatter(lambda n: qv.at[n], sv, x, "dp", xends, 1, 1)
    u1.start()
    v1.start()

    def weight_grads(h):
        begin = sum(cuts[:h])
        width = cuts[h]
        both = dot(gx[h][...].reshape(total, width), dcat, TN).astype(BF16)
        gg[begin : begin + width, :] = both[:, 0:128]
        gu[begin : begin + width, :] = both[:, 128:256]
        gd[begin : begin + width, :] = dot(gc[h][...].reshape(total, width), hidden, TN).astype(BF16)

    weight_grads(0)
    u1.forward()
    v1.forward()
    for h in range(1, parts):
        weight_grads(h)
    stores = [
        pltpu.make_async_copy(gg, gg_hbm, osem.at[0]),
        pltpu.make_async_copy(gu, gu_hbm, osem.at[1]),
        pltpu.make_async_copy(gd, gd_hbm, osem.at[2]),
    ]
    for store in stores:
        store.start()
    qu[...] = u1.finish().astype(BF16)
    u2.start()
    qv[...] = v1.finish().astype(BF16)
    v2.start()
    u2.forward()
    v2.forward()

    back[0:32, :] = u2.finish()
    back[32:64, :] = v2.finish()
    for m in range(32):
        ts[m] = back[2 * m : 2 * m + 2, :].astype(BF16)
    for plane in range(4):
        for i in range(4):
            to = (z - shift(i, plane) + nz) % nz
            for core in range(2):
                base = (plane * 4 + i) * 2
                far = pltpu.make_async_remote_copy(
                    ts.at[base + core], tr.at[base + c], ts_sem, tr_sem,
                    device_id={"expert": to * 2 + core}, device_id_type=MESH,
                )
                if shift(i, plane) == 0:

                    @pl.when(c == core)
                    def _():
                        pltpu.make_async_copy(ts.at[base + core], tr.at[base + c], tr_sem).start()

                    @pl.when(c != core)
                    def _():
                        far.start()
                else:
                    far.start()

    r = lax.broadcasted_iota(jnp.int32, (64, 1), 0)
    home, _ = pick(idt, gvt, z, nz, (r // 4) % 4, r // 16, (r // 2) % 2, r % 2)
    wait(tr, tr_sem)
    for m in range(32):
        back[2 * m : 2 * m + 2, :] = tr[m].astype(F32)
    gi_ref[...] = dot(home.astype(BF16), back[...].astype(BF16), TN).astype(BF16)

    for h in range(parts):

        @pl.when(y == 0)
        def _():
            wait(sb[h].at[0:7], zs.at[h])

        @pl.when(y != 0)
        def _():
            wait(sb[h], zs.at[h])

        run(first[h], "sent")
        run(second[h], "sent")
    for s in (u1, v1, u2, v2):
        s.sent()
    wait(ts.at[0:31], ts_sem)
    for store in stores:
        store.wait()


def local(inputs, cotangent, expert_ids, gate_values, w_gate, w_up, w_down):
    tokens, model = inputs.shape
    nz = lax.axis_size("expert") // 2
    hidden = w_gate.shape[2]
    quarter = model // 4
    cuts = (1536, model - 1536)
    vmem = pl.BlockSpec(memory_space=pltpu.VMEM)
    anywhere = pl.BlockSpec(memory_space=pl.ANY)
    scratch = [pltpu.VMEM((8, 4, w), BF16) for w in cuts]
    scratch += [pltpu.VMEM((8, 4, w), BF16) for w in cuts]
    scratch += [pltpu.VMEM((4, 4, 16, w), BF16) for w in cuts]
    scratch += [pltpu.VMEM((4, 4, 16, w), BF16) for w in cuts]
    scratch += [
        pltpu.VMEM((model, 2 * hidden), BF16),
        pltpu.VMEM((model, hidden), BF16),
        pltpu.VMEM((model, hidden), BF16),
        pltpu.VMEM((model, hidden), BF16),
        pltpu.VMEM((model, hidden), BF16),
        pltpu.VMEM((32, max(cuts)), F32),
        pltpu.VMEM((4, 4, 32, quarter), BF16),
        pltpu.VMEM((4, 4, 32, quarter), BF16),
        pltpu.VMEM((3, 4, 32, quarter), BF16),
        pltpu.VMEM((3, 4, 32, quarter), BF16),
        pltpu.VMEM((4, 32, quarter), BF16),
        pltpu.VMEM((4, 32, quarter), BF16),
        pltpu.VMEM((3, 32, quarter), BF16),
        pltpu.VMEM((3, 32, quarter), BF16),
        pltpu.VMEM((64, quarter), F32),
        pltpu.VMEM((32, 2, quarter), BF16),
        pltpu.VMEM((32, 2, quarter), BF16),
        pltpu.SemaphoreType.DMA((len(cuts),)),
        pltpu.SemaphoreType.DMA((len(cuts),)),
        pltpu.SemaphoreType.DMA((len(cuts), 2, 2, 3)),
        pltpu.SemaphoreType.DMA((len(cuts), 2, 2, 3)),
        pltpu.SemaphoreType.DMA((2, 2, 3)),
        pltpu.SemaphoreType.DMA((2, 2, 3)),
        pltpu.SemaphoreType.DMA,
        pltpu.SemaphoreType.DMA,
        pltpu.SemaphoreType.DMA((3,)),
        pltpu.SemaphoreType.DMA((3,)),
    ]
    grad = jax.ShapeDtypeStruct((model, hidden), BF16)
    gi, gg, gu, gd = pl.pallas_call(
        functools.partial(body, cuts, nz),
        out_shape=(jax.ShapeDtypeStruct((tokens, quarter), BF16), grad, grad, grad),
        in_specs=[vmem] * 4 + [anywhere] * 3,
        out_specs=(vmem, anywhere, anywhere, anywhere),
        scratch_shapes=scratch,
        compiler_params=pltpu.CompilerParams(
            collective_id=0, has_side_effects=True, vmem_limit_bytes=56 * 1024 * 1024
        ),
    )(
        inputs,
        cotangent,
        expert_ids.T,
        gate_values.T,
        w_gate[0],
        w_up[0],
        w_down[0].T,
    )
    return gi, gg[None], gu[None], gd.T[None]


def solution(mesh):
    in_specs = (
        P(("expert", "dp"), None),
        P(("expert", "dp"), None),
        P(("expert", "dp"), None),
        P(("expert", "dp"), None),
        P("expert", None, ("helper", "dp")),
        P("expert", None, ("helper", "dp")),
        P("expert", ("helper", "dp"), None),
    )
    out_specs = (
        P(("expert", "dp"), "helper"),
        P("expert", None, ("helper", "dp")),
        P("expert", None, ("helper", "dp")),
        P("expert", ("helper", "dp"), None),
    )
    return jax.shard_map(local, mesh=mesh, in_specs=in_specs, out_specs=out_specs, check_vma=False)
```

```python
import functools

import jax
import jax.numpy as jnp
from jax import lax
from jax.experimental import pallas as pl
from jax.experimental.pallas import tpu as pltpu
from jax.sharding import PartitionSpec as P

CAP = 2
MESH = pl.DeviceIdType.MESH
F32 = jnp.float32
BF16 = jnp.bfloat16
NT = (((1,), (1,)), ((), ()))
TN = (((0,), (0,)), ((), ()))
NN = (((1,), (0,)), ((), ()))


def dot(a, b, dims=NN):
    return lax.dot_general(a, b, dims, preferred_element_type=F32)


def shift(i, y):
    return (1 + y, 8 - y, -y, y - 7)[i]


def pick_shift(i, y):
    return jnp.where(i == 0, 1 + y, jnp.where(i == 1, 8 - y, jnp.where(i == 2, -y, y - 7)))


def pick(idt, gvt, z, nz, i, y, core, j):
    far = z + pick_shift(i, y)
    far = jnp.where(far < 0, far + nz, jnp.where(far >= nz, far - nz, far))
    expert = far * 2 + core
    tokens = idt.shape[1]
    hits = [(idt[k : k + 1, :] == expert) for k in range(idt.shape[0])]
    named = functools.reduce(lambda a, b: a + b, [h.astype(F32) for h in hits])
    row = lax.broadcasted_iota(jnp.int32, (tokens, tokens), 0)
    col = lax.broadcasted_iota(jnp.int32, (tokens, tokens), 1)
    before = dot(named.astype(BF16), (row < col).astype(BF16))
    chosen = jnp.where(before == j.astype(F32), named, 0.0)
    weight = functools.reduce(lambda a, b: a + b, [h.astype(F32) * gvt[k : k + 1, :] for k, h in enumerate(hits)])
    return chosen, jnp.sum(chosen * weight, axis=1, keepdims=True)


def body(cuts, nz, x_hbm, c_hbm, idt_hbm, gvt_hbm, wg_hbm, wu_hbm, wd_hbm, gi_ref, gg_hbm, gu_hbm, gd_hbm, *rest):
    parts = len(cuts)
    sb, rb, gx, gc = (rest[n * parts : (n + 1) * parts] for n in range(4))
    (x_ref, c_ref, idt_ref, gvt_ref, wcat, wd, gg, gu, gd, stage, pu, pv, ru, rv, qu, qv, su, sv, back, ts, tr,
     zs, zr, ags, agr, rss, rsr, ts_sem, tr_sem, isem, wsem, osem) = rest[4 * parts :]
    e = lax.axis_index("expert")
    y = lax.axis_index("helper")
    x = lax.axis_index("dp")
    ne = 2 * nz
    z = e // 2
    c = e % 2
    model = x_hbm.shape[1]
    quarter = model // 4

    def ring(me):
        return (me + 1 + 2 * c) % 4, (me + 3 - 2 * c) % 4, (me + 2) % 4

    xa, xb, xo = ring(x)
    ya, yb, yo = ring(y)

    barrier = pltpu.get_barrier_semaphore()

    @pl.loop(1, ne)
    def _(n):
        pl.semaphore_signal(barrier, inc=1, device_id={"expert": (e + n) % ne}, device_id_type=MESH)

    for other in (xa, xb, xo):
        pl.semaphore_signal(barrier, inc=1, device_id={"dp": other}, device_id_type=MESH)
    for other in (ya, yb, yo):
        pl.semaphore_signal(barrier, inc=1, device_id={"helper": other}, device_id_type=MESH)

    fetches = [
        pltpu.make_async_copy(idt_hbm, idt_ref, isem.at[0]),
        pltpu.make_async_copy(gvt_hbm, gvt_ref, isem.at[1]),
        pltpu.make_async_copy(x_hbm, x_ref, isem.at[2]),
        pltpu.make_async_copy(c_hbm, c_ref, isem.at[3]),
    ]
    for fetch in fetches:
        fetch.start()
    loads = [
        pltpu.make_async_copy(wg_hbm, wcat.at[:, 0:128], wsem.at[0]),
        pltpu.make_async_copy(wu_hbm, wcat.at[:, 128:256], wsem.at[1]),
        pltpu.make_async_copy(wd_hbm, wd, wsem.at[2]),
    ]
    for load in loads:
        load.start()
    for fetch in fetches:
        fetch.wait()

    idt = idt_ref[...]
    gvt = gvt_ref[...]
    r = lax.broadcasted_iota(jnp.int32, (32, 1), 0)
    half = (r // 2) % 2
    chosen, gate = pick(idt, gvt, z, nz, r // 8, y, (r // 4) % 2, r % 2)
    pick_x = jnp.where(half == 0, chosen, 0.0).astype(BF16)
    pick_c = jnp.where(half == 1, chosen, 0.0).astype(BF16)
    start = 0
    for h, width in enumerate(cuts):
        rows = dot(pick_x, x_ref[:, start : start + width]) + gate * dot(pick_c, c_ref[:, start : start + width])
        for s in range(8):
            sb[h][s] = rows[4 * s : 4 * s + 4, :].astype(BF16)
        start += width

    pl.semaphore_wait(barrier, ne - 1 + 6)

    def wait(ref, sem):
        pltpu.make_async_copy(ref, ref, sem).wait()

    for h in range(parts):
        for i in (1, 3, 0, 2):
            to = (z + shift(i, y) + nz) % nz
            for core in range(2):
                s = 2 * i + core
                far = pltpu.make_async_remote_copy(
                    sb[h].at[s], rb[h].at[2 * i + c], zs.at[h], zr.at[h],
                    device_id={"expert": to * 2 + core}, device_id_type=MESH,
                )
                if i == 2:
                    own = (y == 0) & (c == core)

                    @pl.when(own)
                    def _():
                        pltpu.make_async_copy(sb[h].at[s], rb[h].at[2 * i + c], zr.at[h]).start()

                    @pl.when(jnp.logical_not(own))
                    def _():
                        far.start()
                else:
                    far.start()

    class Gather:
        def __init__(self, view, me, axis, ends, h, a, phase):
            self.view, self.me, self.axis = view, me, axis
            self.ahead, self.behind, self.opposite = ends
            self.ss = [ags.at[h, a, phase, n] for n in range(3)]
            self.rs = [agr.at[h, a, phase, n] for n in range(3)]

        def copy(self, at, n, to):
            return pltpu.make_async_remote_copy(
                self.view(at), self.view(at), self.ss[n], self.rs[n],
                device_id={self.axis: to}, device_id_type=MESH,
            )

        def start(self):
            self.copy(self.me, 0, self.ahead).start()
            self.copy(self.me, 1, self.behind).start()

        def forward(self):
            wait(self.view(self.behind), self.rs[0])
            self.copy(self.behind, 2, self.ahead).start()

        def finish(self):
            wait(self.view(self.ahead), self.rs[1])
            wait(self.view(self.opposite), self.rs[2])

        def sent(self):
            wait(self.view(self.me), self.ss[0])
            wait(self.view(self.me), self.ss[1])
            wait(self.view(self.behind), self.ss[2])

    class Direct(Gather):
        def start(self):
            for n, to in enumerate((self.ahead, self.behind, self.opposite)):
                self.copy(self.me, n, to).start()

        def take(self, n):
            wait(self.view((self.behind, self.ahead, self.opposite)[n]), self.rs[n])

        def sent(self):
            for n in range(3):
                wait(self.view(self.me), self.ss[n])

    xends, yends = (xa, xb, xo), (ya, yb, yo)
    first = [
        (Direct(lambda n, h=h: gx[h].at[n, y], x, "dp", xends, h, 0, 4),
         Direct(lambda n, h=h: gc[h].at[x, n], y, "helper", yends, h, 1, 4))
        for h in range(parts)
    ]
    xroles, yroles = (x, xb, xa, xo), (y, yb, ya, yo)
    second = [
        [(Gather(lambda n, h=h, k=k: gx[h].at[xroles[k], n], y, "helper", yends, h, 0, k),
          Gather(lambda n, h=h, k=k: gc[h].at[n, yroles[k]], x, "dp", xends, h, 1, k))
         for k in range(4)]
        for h in range(parts)
    ]

    def arrive(h):
        wait(rb[h], zr.at[h])
        width = cuts[h]
        for s in range(8):
            rows = rb[h][s].astype(F32)
            stage[2 * s : 2 * s + 2, 0:width] = rows[0:2]
            stage[16 + 2 * s : 18 + 2 * s, 0:width] = rows[2:4]
        gx[h][x, y] = stage[0:16, 0:width].astype(BF16)
        gc[h][x, y] = stage[16:32, 0:width].astype(BF16)
        run(first[h], "start")
        run(second[h][0], "start")

    def run(group, what, *args):
        for g in group:
            getattr(g, what)(*args)

    def pass_on(h):
        for group in second[h]:
            run(group, "forward")

    for h in range(parts):
        arrive(h)
        for n in range(3):
            run(first[h], "take", n)
            run(second[h][n + 1], "start")
        if 0 < h < parts - 1:
            pass_on(h - 1)

    total = 256
    pre = jnp.zeros((total, 256), F32)
    d_hidden = jnp.zeros((total, 128), F32)
    for load in loads:
        load.wait()
    for h in range(parts):
        if h >= max(parts - 2, 0) or parts == 1:
            pass_on(h)
        for group in second[h]:
            run(group, "finish")
        width = cuts[h]
        start = sum(cuts[:h])
        pre = pre + dot(gx[h][...].reshape(total, width), wcat[start : start + width, :])
        d_hidden = d_hidden + dot(gc[h][...].reshape(total, width), wd[start : start + width, :])

    gate_pre = pre[:, 0:128]
    up1 = pre[:, 128:256] + 1.0
    sig = jax.nn.sigmoid(1.702 * gate_pre)
    activated = gate_pre * sig
    hidden = (up1 * activated).astype(BF16)
    d_up = (d_hidden * activated).astype(BF16)
    d_gate = (d_hidden * up1 * (sig + 1.702 * gate_pre * sig * (1.0 - sig))).astype(BF16)
    dcat = jnp.concatenate([d_gate, d_up], axis=1)

    for q in range(4):
        part = dot(dcat, wcat[quarter * q : quarter * (q + 1), :], NT)
        for n in range(4):
            for k in range(2):
                at = 64 * n + 16 * k
                pu[k, n, q] = part[at : at + 16, :].astype(BF16)
                pv[k, n, q] = part[at + 32 : at + 48, :].astype(BF16)

    class Scatter:
        def __init__(self, view, land, me, axis, ends, k, a, phase):
            self.view, self.land, self.me, self.axis = view, land, me, axis
            self.ahead, self.behind, self.opposite = ends
            self.ss = [rss.at[k, a, phase, n] for n in range(3)]
            self.rs = [rsr.at[k, a, phase, n] for n in range(3)]

        def copy(self, at, n, to):
            return pltpu.make_async_remote_copy(
                self.view(at), self.land.at[n], self.ss[n], self.rs[n],
                device_id={self.axis: to}, device_id_type=MESH,
            )

        def start(self):
            self.copy(self.opposite, 0, self.ahead).start()
            self.copy(self.behind, 1, self.behind).start()

        def forward(self):
            wait(self.land.at[0], self.rs[0])
            ref = self.view(self.ahead)
            ref[...] = (ref[...].astype(F32) + self.land[0].astype(F32)).astype(BF16)
            self.copy(self.ahead, 2, self.ahead).start()

        def finish(self):
            wait(self.land.at[1], self.rs[1])
            wait(self.land.at[2], self.rs[2])
            return self.view(self.me)[...].astype(F32) + self.land[1].astype(F32) + self.land[2].astype(F32)

        def sent(self):
            for n in range(3):
                wait(self.land.at[n], self.ss[n])

    class DirectScatter(Scatter):
        def start(self):
            for n, to in enumerate((self.ahead, self.behind, self.opposite)):
                self.copy(to, n, to).start()

        def finish(self):
            for n in range(3):
                wait(self.land.at[n], self.rs[n])
            terms = [self.land[n].astype(F32) for n in range(3)]
            return self.view(self.me)[...].astype(F32) + terms[0] + terms[1] + terms[2]

    one = [
        (Scatter(lambda n, k=k: pu.at[k, n], ru.at[k], x, "dp", xends, k, 0, 0),
         Scatter(lambda n, k=k: pv.at[k, :, n], rv.at[k], y, "helper", yends, k, 1, 0))
        for k in range(2)
    ]
    two = [
        (DirectScatter(lambda n, k=k: qu.at[k, n], su.at[k], y, "helper", yends, k, 0, 1),
         DirectScatter(lambda n, k=k: qv.at[k, n], sv.at[k], x, "dp", xends, k, 1, 1))
        for k in range(2)
    ]
    for k in range(2):
        run(one[k], "start")

    def weight_grads(h, begin, end):
        cut = slice(begin, end)
        both = dot(gx[h][:, :, :, cut].reshape(total, end - begin), dcat, TN).astype(BF16)
        gg[cut, :] = both[:, 0:128]
        gu[cut, :] = both[:, 128:256]
        gd[cut, :] = dot(gc[h][:, :, :, cut].reshape(total, end - begin), hidden, TN).astype(BF16)

    def give_back(plane, rows):
        back[16 * plane : 16 * plane + 16, :] = rows
        for i in range(4):
            to = (z - shift(i, plane) + nz) % nz
            for core in range(2):
                base = (plane * 4 + i) * 2
                m = base + core
                ts[m] = back[2 * m : 2 * m + 2, :].astype(BF16)
                far = pltpu.make_async_remote_copy(
                    ts.at[m], tr.at[base + c], ts_sem, tr_sem,
                    device_id={"expert": to * 2 + core}, device_id_type=MESH,
                )
                if shift(i, plane) == 0:

                    @pl.when(c == core)
                    def _():
                        pltpu.make_async_copy(ts.at[m], tr.at[base + c], tr_sem).start()

                    @pl.when(c != core)
                    def _():
                        far.start()
                else:
                    far.start()

    weight_grads(0, 0, 1536)
    run(one[0], "forward")
    run(one[1], "forward")
    weight_grads(0, 1536, model)
    for k in range(2):
        qu[k] = one[k][0].finish().astype(BF16)
        two[k][0].start()
        qv[k] = one[k][1].finish().astype(BF16)
        two[k][1].start()
    for k in range(2):
        give_back(k, two[k][0].finish())
        give_back(2 + k, two[k][1].finish())
    stores = [
        pltpu.make_async_copy(gg, gg_hbm, osem.at[0]),
        pltpu.make_async_copy(gu, gu_hbm, osem.at[1]),
        pltpu.make_async_copy(gd, gd_hbm, osem.at[2]),
    ]
    for store in stores:
        store.start()

    r = lax.broadcasted_iota(jnp.int32, (64, 1), 0)
    home, _ = pick(idt, gvt, z, nz, (r // 4) % 4, r // 16, (r // 2) % 2, r % 2)
    wait(tr, tr_sem)
    for m in range(32):
        back[2 * m : 2 * m + 2, :] = tr[m].astype(F32)
    gi_ref[...] = dot(home.astype(BF16), back[...].astype(BF16), TN).astype(BF16)

    for h in range(parts):
        @pl.when(y == 0)
        def _():
            wait(sb[h].at[0:7], zs.at[h])

        @pl.when(y != 0)
        def _():
            wait(sb[h], zs.at[h])

        run(first[h], "sent")
        for group in second[h]:
            run(group, "sent")
    for k in range(2):
        run(one[k], "sent")
        run(two[k], "sent")
    wait(ts.at[0:31], ts_sem)
    for store in stores:
        store.wait()


def hand_over(*refs):
    ins, outs, held, sems = refs[0:4], refs[4:8], refs[8:12], refs[12]
    loads = [pltpu.make_async_copy(ins[n], held[n], sems.at[0, n]) for n in range(4)]
    stores = [pltpu.make_async_copy(held[n], outs[n], sems.at[1, n]) for n in range(4)]
    for load in loads:
        load.start()
    for load, store in zip(loads, stores):
        load.wait()
        store.start()
    for store in stores:
        store.wait()


def local(inputs, cotangent, expert_ids, gate_values, w_gate, w_up, w_down):
    tokens, model = inputs.shape
    nz = lax.axis_size("expert") // 2
    hidden = w_gate.shape[2]
    quarter = model // 4
    cuts = (model,)
    vmem = pl.BlockSpec(memory_space=pltpu.VMEM)
    anywhere = pl.BlockSpec(memory_space=pl.ANY)
    scratch = [pltpu.VMEM((8, 4, w), BF16) for w in cuts]
    scratch += [pltpu.VMEM((8, 4, w), BF16) for w in cuts]
    scratch += [pltpu.VMEM((4, 4, 16, w), BF16) for w in cuts]
    scratch += [pltpu.VMEM((4, 4, 16, w), BF16) for w in cuts]
    scratch += [
        pltpu.VMEM((tokens, model), BF16),
        pltpu.VMEM((tokens, model), BF16),
        pltpu.VMEM(expert_ids.shape[::-1], expert_ids.dtype),
        pltpu.VMEM(gate_values.shape[::-1], gate_values.dtype),
        pltpu.VMEM((model, 2 * hidden), BF16),
        pltpu.VMEM((model, hidden), BF16),
        pltpu.VMEM((model, hidden), BF16),
        pltpu.VMEM((model, hidden), BF16),
        pltpu.VMEM((model, hidden), BF16),
        pltpu.VMEM((32, max(cuts)), F32),
        pltpu.VMEM((2, 4, 4, 16, quarter), BF16),
        pltpu.VMEM((2, 4, 4, 16, quarter), BF16),
        pltpu.VMEM((2, 3, 4, 16, quarter), BF16),
        pltpu.VMEM((2, 3, 4, 16, quarter), BF16),
        pltpu.VMEM((2, 4, 16, quarter), BF16),
        pltpu.VMEM((2, 4, 16, quarter), BF16),
        pltpu.VMEM((2, 3, 16, quarter), BF16),
        pltpu.VMEM((2, 3, 16, quarter), BF16),
        pltpu.VMEM((64, quarter), F32),
        pltpu.VMEM((32, 2, quarter), BF16),
        pltpu.VMEM((32, 2, quarter), BF16),
        pltpu.SemaphoreType.DMA((len(cuts),)),
        pltpu.SemaphoreType.DMA((len(cuts),)),
        pltpu.SemaphoreType.DMA((len(cuts), 2, 5, 3)),
        pltpu.SemaphoreType.DMA((len(cuts), 2, 5, 3)),
        pltpu.SemaphoreType.DMA((2, 2, 2, 3)),
        pltpu.SemaphoreType.DMA((2, 2, 2, 3)),
        pltpu.SemaphoreType.DMA,
        pltpu.SemaphoreType.DMA,
        pltpu.SemaphoreType.DMA((4,)),
        pltpu.SemaphoreType.DMA((3,)),
        pltpu.SemaphoreType.DMA((3,)),
    ]
    grad = jax.ShapeDtypeStruct((model, hidden), BF16)
    grads = pl.pallas_call(
        functools.partial(body, cuts, nz),
        out_shape=(jax.ShapeDtypeStruct((tokens, quarter), BF16), grad, grad, grad),
        in_specs=[anywhere] * 7,
        out_specs=(vmem, anywhere, anywhere, anywhere),
        scratch_shapes=scratch,
        compiler_params=pltpu.CompilerParams(
            collective_id=0, has_side_effects=True, vmem_limit_bytes=56 * 1024 * 1024
        ),
    )(
        inputs,
        cotangent,
        expert_ids.T,
        gate_values.T,
        w_gate[0],
        w_up[0],
        w_down[0].T,
    )
    gi, gg, gu, gd = pl.pallas_call(
        hand_over,
        out_shape=tuple(jax.ShapeDtypeStruct(g.shape, g.dtype) for g in grads),
        in_specs=[anywhere] * 4,
        out_specs=(anywhere,) * 4,
        scratch_shapes=[pltpu.VMEM(g.shape, g.dtype) for g in grads] + [pltpu.SemaphoreType.DMA((2, 4))],
    )(*grads)
    return gi, gg[None], gu[None], gd.T[None]


def solution(mesh):
    in_specs = (
        P(("expert", "dp"), None),
        P(("expert", "dp"), None),
        P(("expert", "dp"), None),
        P(("expert", "dp"), None),
        P("expert", None, ("helper", "dp")),
        P("expert", None, ("helper", "dp")),
        P("expert", ("helper", "dp"), None),
    )
    out_specs = (
        P(("expert", "dp"), "helper"),
        P("expert", None, ("helper", "dp")),
        P("expert", None, ("helper", "dp")),
        P("expert", ("helper", "dp"), None),
    )
    return jax.shard_map(local, mesh=mesh, in_specs=in_specs, out_specs=out_specs, check_vma=False)
```

```python
import functools

import jax
import jax.numpy as jnp
from jax import lax
from jax.experimental import pallas as pl
from jax.experimental.pallas import tpu as pltpu
from jax.sharding import PartitionSpec as P

CAP = 2
MESH = pl.DeviceIdType.MESH
F32 = jnp.float32
BF16 = jnp.bfloat16
NT = (((1,), (1,)), ((), ()))
TN = (((0,), (0,)), ((), ()))
NN = (((1,), (0,)), ((), ()))


def dot(a, b, dims=NN):
    return lax.dot_general(a, b, dims, preferred_element_type=F32)


def shift(i, y):
    return (1 + y, 8 - y, -y, y - 7)[i]


def pick_shift(i, y):
    return jnp.where(i == 0, 1 + y, jnp.where(i == 1, 8 - y, jnp.where(i == 2, -y, y - 7)))


def pick(idt, gvt, z, nz, i, y, core, j):
    far = z + pick_shift(i, y)
    far = jnp.where(far < 0, far + nz, jnp.where(far >= nz, far - nz, far))
    expert = far * 2 + core
    tokens = idt.shape[1]
    hits = [(idt[k : k + 1, :] == expert) for k in range(idt.shape[0])]
    named = functools.reduce(lambda a, b: a + b, [h.astype(F32) for h in hits])
    row = lax.broadcasted_iota(jnp.int32, (tokens, tokens), 0)
    col = lax.broadcasted_iota(jnp.int32, (tokens, tokens), 1)
    before = dot(named.astype(BF16), (row < col).astype(BF16))
    chosen = jnp.where(before == j.astype(F32), named, 0.0)
    weight = functools.reduce(lambda a, b: a + b, [h.astype(F32) * gvt[k : k + 1, :] for k, h in enumerate(hits)])
    return chosen, jnp.sum(chosen * weight, axis=1, keepdims=True)


def body(cuts, nz, x_hbm, c_hbm, idt_hbm, gvt_hbm, wg_hbm, wu_hbm, wd_hbm, gi_ref, gg, gu, gd, *rest):
    parts = len(cuts)
    sb, rb, gx, gc = (rest[n * parts : (n + 1) * parts] for n in range(4))
    (x_ref, c_ref, idt_ref, gvt_ref, wcat, wd, stage, pu, pv, ru, rv, qu, qv, su, sv, back, ts, tr,
     zs, zr, ags, agr, rss, rsr, ts_sem, tr_sem, isem, wsem) = rest[4 * parts :]
    e = lax.axis_index("expert")
    y = lax.axis_index("helper")
    x = lax.axis_index("dp")
    ne = 2 * nz
    z = e // 2
    c = e % 2
    model = x_hbm.shape[1]
    quarter = model // 4

    def ring(me):
        return (me + 1 + 2 * c) % 4, (me + 3 - 2 * c) % 4, (me + 2) % 4

    xa, xb, xo = ring(x)
    ya, yb, yo = ring(y)

    barrier = pltpu.get_barrier_semaphore()

    for n in sorted(range(1, ne), key=lambda n: -min(n, ne - n)):
        pl.semaphore_signal(barrier, inc=1, device_id={"expert": (e + n) % ne}, device_id_type=MESH)

    for other in (xa, xb, xo):
        pl.semaphore_signal(barrier, inc=1, device_id={"dp": other}, device_id_type=MESH)
    for other in (ya, yb, yo):
        pl.semaphore_signal(barrier, inc=1, device_id={"helper": other}, device_id_type=MESH)

    fetches = [
        pltpu.make_async_copy(idt_hbm, idt_ref, isem.at[0]),
        pltpu.make_async_copy(gvt_hbm, gvt_ref, isem.at[1]),
        pltpu.make_async_copy(x_hbm, x_ref, isem.at[2]),
        pltpu.make_async_copy(c_hbm, c_ref, isem.at[3]),
    ]
    for fetch in fetches:
        fetch.start()
    loads = [
        pltpu.make_async_copy(wg_hbm, wcat.at[:, 0:128], wsem.at[0]),
        pltpu.make_async_copy(wu_hbm, wcat.at[:, 128:256], wsem.at[1]),
        pltpu.make_async_copy(wd_hbm, wd, wsem.at[2]),
    ]
    for load in loads:
        load.start()
    for fetch in fetches:
        fetch.wait()

    idt = idt_ref[...]
    gvt = gvt_ref[...]
    r = lax.broadcasted_iota(jnp.int32, (32, 1), 0)
    half = (r // 2) % 2
    chosen, gate = pick(idt, gvt, z, nz, r // 8, y, (r // 4) % 2, r % 2)
    pick_x = jnp.where(half == 0, chosen, 0.0).astype(BF16)
    pick_c = jnp.where(half == 1, chosen, 0.0).astype(BF16)
    start = 0
    for h, width in enumerate(cuts):
        rows = dot(pick_x, x_ref[:, start : start + width]) + gate * dot(pick_c, c_ref[:, start : start + width])
        for s in range(8):
            sb[h][s] = rows[4 * s : 4 * s + 4, :].astype(BF16)
        start += width

    pl.semaphore_wait(barrier, ne - 1 + 6)

    def wait(ref, sem):
        pltpu.make_async_copy(ref, ref, sem).wait()

    for h in range(parts):
        for i in (1, 3, 0, 2):
            to = (z + shift(i, y) + nz) % nz
            for core in range(2):
                s = 2 * i + core
                far = pltpu.make_async_remote_copy(
                    sb[h].at[s], rb[h].at[2 * i + c], zs.at[h], zr.at[h],
                    device_id={"expert": to * 2 + core}, device_id_type=MESH,
                )
                if i == 2:
                    own = (y == 0) & (c == core)

                    @pl.when(own)
                    def _():
                        pltpu.make_async_copy(sb[h].at[s], rb[h].at[2 * i + c], zr.at[h]).start()

                    @pl.when(jnp.logical_not(own))
                    def _():
                        far.start()
                else:
                    far.start()

    class Gather:
        def __init__(self, view, me, axis, ends, h, a, phase):
            self.view, self.me, self.axis = view, me, axis
            self.ahead, self.behind, self.opposite = ends
            self.ss = [ags.at[h, a, phase, n] for n in range(3)]
            self.rs = [agr.at[h, a, phase, n] for n in range(3)]

        def copy(self, at, n, to):
            return pltpu.make_async_remote_copy(
                self.view(at), self.view(at), self.ss[n], self.rs[n],
                device_id={self.axis: to}, device_id_type=MESH,
            )

        def start(self):
            self.copy(self.me, 0, self.ahead).start()
            self.copy(self.me, 1, self.behind).start()

        def forward(self):
            wait(self.view(self.behind), self.rs[0])
            self.copy(self.behind, 2, self.ahead).start()

        def finish(self):
            wait(self.view(self.ahead), self.rs[1])
            wait(self.view(self.opposite), self.rs[2])

        def sent(self):
            wait(self.view(self.me), self.ss[0])
            wait(self.view(self.me), self.ss[1])
            wait(self.view(self.behind), self.ss[2])

    class Direct(Gather):
        def start(self):
            for n, to in enumerate((self.ahead, self.behind, self.opposite)):
                self.copy(self.me, n, to).start()

        def take(self, n):
            wait(self.view((self.behind, self.ahead, self.opposite)[n]), self.rs[n])

        def sent(self):
            for n in range(3):
                wait(self.view(self.me), self.ss[n])

    xends, yends = (xa, xb, xo), (ya, yb, yo)
    first = [
        (Direct(lambda n, h=h: gx[h].at[n, y], x, "dp", xends, h, 0, 4),
         Direct(lambda n, h=h: gc[h].at[x, n], y, "helper", yends, h, 1, 4))
        for h in range(parts)
    ]
    xroles, yroles = (x, xb, xa, xo), (y, yb, ya, yo)
    second = [
        [(Gather(lambda n, h=h, k=k: gx[h].at[xroles[k], n], y, "helper", yends, h, 0, k),
          Gather(lambda n, h=h, k=k: gc[h].at[n, yroles[k]], x, "dp", xends, h, 1, k))
         for k in range(4)]
        for h in range(parts)
    ]

    def arrive(h):
        wait(rb[h], zr.at[h])
        width = cuts[h]
        for s in range(8):
            rows = rb[h][s].astype(F32)
            stage[2 * s : 2 * s + 2, 0:width] = rows[0:2]
            stage[16 + 2 * s : 18 + 2 * s, 0:width] = rows[2:4]
        gx[h][x, y] = stage[0:16, 0:width].astype(BF16)
        gc[h][x, y] = stage[16:32, 0:width].astype(BF16)
        run(first[h], "start")
        run(second[h][0], "start")

    def run(group, what, *args):
        for g in group:
            getattr(g, what)(*args)

    def pass_on(h):
        for group in second[h]:
            run(group, "forward")

    for h in range(parts):
        arrive(h)
        for n in range(3):
            run(first[h], "take", n)
            run(second[h][n + 1], "start")
        if 0 < h < parts - 1:
            pass_on(h - 1)

    total = 256
    pre = jnp.zeros((total, 256), F32)
    d_hidden = jnp.zeros((total, 128), F32)
    for load in loads:
        load.wait()
    for h in range(parts):
        if h >= max(parts - 2, 0) or parts == 1:
            pass_on(h)
        for group in second[h]:
            run(group, "finish")
        width = cuts[h]
        start = sum(cuts[:h])
        pre = pre + dot(gx[h][...].reshape(total, width), wcat[start : start + width, :])
        d_hidden = d_hidden + dot(gc[h][...].reshape(total, width), wd[start : start + width, :])

    gate_pre = pre[:, 0:128]
    up1 = pre[:, 128:256] + 1.0
    sig = jax.nn.sigmoid(1.702 * gate_pre)
    activated = gate_pre * sig
    hidden = (up1 * activated).astype(BF16)
    d_up = (d_hidden * activated).astype(BF16)
    d_gate = (d_hidden * up1 * (sig + 1.702 * gate_pre * sig * (1.0 - sig))).astype(BF16)
    dcat = jnp.concatenate([d_gate, d_up], axis=1)

    for q in range(4):
        part = dot(dcat, wcat[quarter * q : quarter * (q + 1), :], NT)
        for n in range(4):
            for k in range(2):
                at = 64 * n + 16 * k
                pu[k, n, q] = part[at : at + 16, :].astype(BF16)
                pv[k, n, q] = part[at + 32 : at + 48, :].astype(BF16)

    class Scatter:
        def __init__(self, view, land, me, axis, ends, k, a, phase):
            self.view, self.land, self.me, self.axis = view, land, me, axis
            self.ahead, self.behind, self.opposite = ends
            self.ss = [rss.at[k, a, phase, n] for n in range(3)]
            self.rs = [rsr.at[k, a, phase, n] for n in range(3)]

        def copy(self, at, n, to):
            return pltpu.make_async_remote_copy(
                self.view(at), self.land.at[n], self.ss[n], self.rs[n],
                device_id={self.axis: to}, device_id_type=MESH,
            )

        def start(self):
            self.copy(self.opposite, 0, self.ahead).start()
            self.copy(self.behind, 1, self.behind).start()

        def forward(self):
            wait(self.land.at[0], self.rs[0])
            ref = self.view(self.ahead)
            ref[...] = (ref[...].astype(F32) + self.land[0].astype(F32)).astype(BF16)
            self.copy(self.ahead, 2, self.ahead).start()

        def finish(self):
            wait(self.land.at[1], self.rs[1])
            wait(self.land.at[2], self.rs[2])
            return self.view(self.me)[...].astype(F32) + self.land[1].astype(F32) + self.land[2].astype(F32)

        def sent(self):
            for n in range(3):
                wait(self.land.at[n], self.ss[n])

    class DirectScatter(Scatter):
        def start(self):
            for n, to in enumerate((self.ahead, self.behind, self.opposite)):
                self.copy(to, n, to).start()

        def finish(self):
            for n in range(3):
                wait(self.land.at[n], self.rs[n])
            terms = [self.land[n].astype(F32) for n in range(3)]
            return self.view(self.me)[...].astype(F32) + terms[0] + terms[1] + terms[2]

    one = [
        (Scatter(lambda n, k=k: pu.at[k, n], ru.at[k], x, "dp", xends, k, 0, 0),
         Scatter(lambda n, k=k: pv.at[k, :, n], rv.at[k], y, "helper", yends, k, 1, 0))
        for k in range(2)
    ]
    two = [
        (DirectScatter(lambda n, k=k: qu.at[k, n], su.at[k], y, "helper", yends, k, 0, 1),
         DirectScatter(lambda n, k=k: qv.at[k, n], sv.at[k], x, "dp", xends, k, 1, 1))
        for k in range(2)
    ]
    for k in range(2):
        run(one[k], "start")

    def weight_grads(h, begin, end):
        cut = slice(begin, end)
        both = dot(gx[h][:, :, :, cut].reshape(total, end - begin), dcat, TN).astype(BF16)
        gg[cut, :] = both[:, 0:128]
        gu[cut, :] = both[:, 128:256]
        gd[cut, :] = dot(gc[h][:, :, :, cut].reshape(total, end - begin), hidden, TN).astype(BF16)

    def give_back(plane, rows):
        back[16 * plane : 16 * plane + 16, :] = rows
        for i in (1, 3, 0, 2):
            to = (z - shift(i, plane) + nz) % nz
            for core in range(2):
                base = (plane * 4 + i) * 2
                m = base + core
                ts[m] = back[2 * m : 2 * m + 2, :].astype(BF16)
                far = pltpu.make_async_remote_copy(
                    ts.at[m], tr.at[base + c], ts_sem, tr_sem,
                    device_id={"expert": to * 2 + core}, device_id_type=MESH,
                )
                if shift(i, plane) == 0:

                    @pl.when(c == core)
                    def _():
                        pltpu.make_async_copy(ts.at[m], tr.at[base + c], tr_sem).start()

                    @pl.when(c != core)
                    def _():
                        far.start()
                else:
                    far.start()

    run(one[0], "forward")
    run(one[1], "forward")
    for k in range(2):
        qu[k] = one[k][0].finish().astype(BF16)
        two[k][0].start()
        qv[k] = one[k][1].finish().astype(BF16)
        two[k][1].start()
    for k in range(2):
        give_back(k, two[k][0].finish())
        give_back(2 + k, two[k][1].finish())
    weight_grads(0, 0, model)
    r = lax.broadcasted_iota(jnp.int32, (64, 1), 0)
    home, _ = pick(idt, gvt, z, nz, (r // 4) % 4, r // 16, (r // 2) % 2, r % 2)
    wait(tr, tr_sem)
    for m in range(32):
        back[2 * m : 2 * m + 2, :] = tr[m].astype(F32)
    gi_ref[...] = dot(home.astype(BF16), back[...].astype(BF16), TN).astype(BF16)

    for h in range(parts):
        @pl.when(y == 0)
        def _():
            wait(sb[h].at[0:7], zs.at[h])

        @pl.when(y != 0)
        def _():
            wait(sb[h], zs.at[h])

        run(first[h], "sent")
        for group in second[h]:
            run(group, "sent")
    for k in range(2):
        run(one[k], "sent")
        run(two[k], "sent")
    wait(ts.at[0:31], ts_sem)


def hand_over(*refs):
    copies = [pltpu.make_async_copy(refs[n], refs[4 + n], refs[8].at[n]) for n in range(4)]
    for copy in copies:
        copy.start()
    for copy in copies:
        copy.wait()


def local(inputs, cotangent, expert_ids, gate_values, w_gate, w_up, w_down):
    tokens, model = inputs.shape
    nz = lax.axis_size("expert") // 2
    hidden = w_gate.shape[2]
    quarter = model // 4
    cuts = (model,)
    vmem = pl.BlockSpec(memory_space=pltpu.VMEM)
    anywhere = pl.BlockSpec(memory_space=pl.ANY)
    scratch = [pltpu.VMEM((8, 4, w), BF16) for w in cuts]
    scratch += [pltpu.VMEM((8, 4, w), BF16) for w in cuts]
    scratch += [pltpu.VMEM((4, 4, 16, w), BF16) for w in cuts]
    scratch += [pltpu.VMEM((4, 4, 16, w), BF16) for w in cuts]
    scratch += [
        pltpu.VMEM((tokens, model), BF16),
        pltpu.VMEM((tokens, model), BF16),
        pltpu.VMEM(expert_ids.shape[::-1], expert_ids.dtype),
        pltpu.VMEM(gate_values.shape[::-1], gate_values.dtype),
        pltpu.VMEM((model, 2 * hidden), BF16),
        pltpu.VMEM((model, hidden), BF16),
        pltpu.VMEM((32, max(cuts)), F32),
        pltpu.VMEM((2, 4, 4, 16, quarter), BF16),
        pltpu.VMEM((2, 4, 4, 16, quarter), BF16),
        pltpu.VMEM((2, 3, 4, 16, quarter), BF16),
        pltpu.VMEM((2, 3, 4, 16, quarter), BF16),
        pltpu.VMEM((2, 4, 16, quarter), BF16),
        pltpu.VMEM((2, 4, 16, quarter), BF16),
        pltpu.VMEM((2, 3, 16, quarter), BF16),
        pltpu.VMEM((2, 3, 16, quarter), BF16),
        pltpu.VMEM((64, quarter), F32),
        pltpu.VMEM((32, 2, quarter), BF16),
        pltpu.VMEM((32, 2, quarter), BF16),
        pltpu.SemaphoreType.DMA((len(cuts),)),
        pltpu.SemaphoreType.DMA((len(cuts),)),
        pltpu.SemaphoreType.DMA((len(cuts), 2, 5, 3)),
        pltpu.SemaphoreType.DMA((len(cuts), 2, 5, 3)),
        pltpu.SemaphoreType.DMA((2, 2, 2, 3)),
        pltpu.SemaphoreType.DMA((2, 2, 2, 3)),
        pltpu.SemaphoreType.DMA,
        pltpu.SemaphoreType.DMA,
        pltpu.SemaphoreType.DMA((4,)),
        pltpu.SemaphoreType.DMA((3,)),
    ]
    grad = pltpu.VMEM((model, hidden), BF16)
    grads = pl.pallas_call(
        functools.partial(body, cuts, nz),
        out_shape=(pltpu.VMEM((tokens, quarter), BF16), grad, grad, grad),
        in_specs=[anywhere] * 7,
        out_specs=(vmem,) * 4,
        scratch_shapes=scratch,
        compiler_params=pltpu.CompilerParams(
            collective_id=0, has_side_effects=True, vmem_limit_bytes=56 * 1024 * 1024
        ),
    )(
        inputs,
        cotangent,
        expert_ids.T,
        gate_values.T,
        w_gate[0],
        w_up[0],
        w_down[0].T,
    )
    gi, gg, gu, gd = pl.pallas_call(
        hand_over,
        out_shape=tuple(jax.ShapeDtypeStruct(g.shape, g.dtype) for g in grads),
        in_specs=[anywhere] * 4,
        out_specs=(anywhere,) * 4,
        scratch_shapes=[pltpu.SemaphoreType.DMA((4,))],
    )(*(pltpu.with_memory_space_constraint(g, pltpu.VMEM) for g in grads))
    return gi, gg[None], gu[None], gd.T[None]


def solution(mesh):
    in_specs = (
        P(("expert", "dp"), None),
        P(("expert", "dp"), None),
        P(("expert", "dp"), None),
        P(("expert", "dp"), None),
        P("expert", None, ("helper", "dp")),
        P("expert", None, ("helper", "dp")),
        P("expert", ("helper", "dp"), None),
    )
    out_specs = (
        P(("expert", "dp"), "helper"),
        P("expert", None, ("helper", "dp")),
        P("expert", None, ("helper", "dp")),
        P("expert", ("helper", "dp"), None),
    )
    return jax.shard_map(local, mesh=mesh, in_specs=in_specs, out_specs=out_specs, check_vma=False)
```

```python
import functools

import jax
import jax.numpy as jnp
from jax import lax
from jax.experimental import pallas as pl
from jax.experimental.pallas import tpu as pltpu
from jax.sharding import PartitionSpec as P

CAP = 2
MESH = pl.DeviceIdType.MESH
F32 = jnp.float32
BF16 = jnp.bfloat16
NT = (((1,), (1,)), ((), ()))
TN = (((0,), (0,)), ((), ()))
NN = (((1,), (0,)), ((), ()))


def dot(a, b, dims=NN):
    return lax.dot_general(a, b, dims, preferred_element_type=F32)


def shift(i, y):
    none = 1 - (y + 3) // 4
    return (y + 4 * none, -y - 4 * none, 8 - y, (y - 8) * (1 - none))[i]


def pick_shift(i, y):
    a, b, c, d = (shift(n, y) for n in range(4))
    return jnp.where(i == 0, a, jnp.where(i == 1, b, jnp.where(i == 2, c, d)))


def pick(idt, gvt, z, nz, i, y, core, j):
    far = z + pick_shift(i, y)
    far = jnp.where(far < 0, far + nz, jnp.where(far >= nz, far - nz, far))
    expert = far * 2 + core
    tokens = idt.shape[1]
    hits = [(idt[k : k + 1, :] == expert) for k in range(idt.shape[0])]
    named = functools.reduce(lambda a, b: a + b, [h.astype(F32) for h in hits])
    row = lax.broadcasted_iota(jnp.int32, (tokens, tokens), 0)
    col = lax.broadcasted_iota(jnp.int32, (tokens, tokens), 1)
    before = dot(named.astype(BF16), (row < col).astype(BF16))
    chosen = jnp.where(before == j.astype(F32), named, 0.0)
    weight = functools.reduce(lambda a, b: a + b, [h.astype(F32) * gvt[k : k + 1, :] for k, h in enumerate(hits)])
    return chosen, jnp.sum(chosen * weight, axis=1, keepdims=True)


def body(cuts, nz, x_hbm, c_hbm, idt_hbm, gvt_hbm, wg_hbm, wu_hbm, wd_hbm, gi_ref, gg, gu, gd, *rest):
    parts = len(cuts)
    sb, rb, gx, gc = (rest[n * parts : (n + 1) * parts] for n in range(4))
    (x_ref, c_ref, idt_ref, gvt_ref, wcat, wd, stage, pu, pv, ru, rv, qu, qv, su, sv, back, ts, tr,
     zs, zr, ags, agr, rss, rsr, ts_sem, tr_sem, isem, wsem) = rest[4 * parts :]
    e = lax.axis_index("expert")
    y = lax.axis_index("helper")
    x = lax.axis_index("dp")
    ne = 2 * nz
    z = e // 2
    c = e % 2
    model = x_hbm.shape[1]
    quarter = model // 4

    def ring(me):
        return (me + 1 + 2 * c) % 4, (me + 3 - 2 * c) % 4, (me + 2) % 4

    xa, xb, xo = ring(x)
    ya, yb, yo = ring(y)

    barrier = pltpu.get_barrier_semaphore()

    for n in sorted(range(1, ne), key=lambda n: -min(n, ne - n)):
        pl.semaphore_signal(barrier, inc=1, device_id={"expert": (e + n) % ne}, device_id_type=MESH)

    for other in (xa, xb, xo):
        pl.semaphore_signal(barrier, inc=1, device_id={"dp": other}, device_id_type=MESH)
    for other in (ya, yb, yo):
        pl.semaphore_signal(barrier, inc=1, device_id={"helper": other}, device_id_type=MESH)

    fetches = [
        pltpu.make_async_copy(idt_hbm, idt_ref, isem.at[0]),
        pltpu.make_async_copy(gvt_hbm, gvt_ref, isem.at[1]),
        pltpu.make_async_copy(x_hbm, x_ref, isem.at[2]),
        pltpu.make_async_copy(c_hbm, c_ref, isem.at[3]),
    ]
    for fetch in fetches:
        fetch.start()
    loads = [
        pltpu.make_async_copy(wg_hbm, wcat.at[:, 0:128], wsem.at[0]),
        pltpu.make_async_copy(wu_hbm, wcat.at[:, 128:256], wsem.at[1]),
        pltpu.make_async_copy(wd_hbm, wd, wsem.at[2]),
    ]
    for load in loads:
        load.start()
    for fetch in fetches:
        fetch.wait()

    idt = idt_ref[...]
    gvt = gvt_ref[...]
    r = lax.broadcasted_iota(jnp.int32, (32, 1), 0)
    half = (r // 2) % 2
    chosen, gate = pick(idt, gvt, z, nz, r // 8, y, (r // 4) % 2, r % 2)
    pick_x = jnp.where(half == 0, chosen, 0.0).astype(BF16)
    pick_c = jnp.where(half == 1, chosen, 0.0).astype(BF16)
    start = 0
    for h, width in enumerate(cuts):
        rows = dot(pick_x, x_ref[:, start : start + width]) + gate * dot(pick_c, c_ref[:, start : start + width])
        for s in range(8):
            sb[h][s] = rows[4 * s : 4 * s + 4, :].astype(BF16)
        start += width

    pl.semaphore_wait(barrier, ne - 1 + 6)

    def wait(ref, sem):
        pltpu.make_async_copy(ref, ref, sem).wait()

    for h in range(parts):
        for i in (2, 3, 0, 1):
            to = (z + shift(i, y) + nz) % nz
            for core in range(2):
                s = 2 * i + core
                far = pltpu.make_async_remote_copy(
                    sb[h].at[s], rb[h].at[2 * i + c], zs.at[h], zr.at[h],
                    device_id={"expert": to * 2 + core}, device_id_type=MESH,
                )
                if i == 3:
                    own = (y == 0) & (c == core)

                    @pl.when(own)
                    def _():
                        pltpu.make_async_copy(sb[h].at[s], rb[h].at[2 * i + c], zr.at[h]).start()

                    @pl.when(jnp.logical_not(own))
                    def _():
                        far.start()
                else:
                    far.start()

    class Gather:
        def __init__(self, view, me, axis, ends, h, a, phase):
            self.view, self.me, self.axis = view, me, axis
            self.ahead, self.behind, self.opposite = ends
            self.ss = [ags.at[h, a, phase, n] for n in range(3)]
            self.rs = [agr.at[h, a, phase, n] for n in range(3)]

        def copy(self, at, n, to):
            return pltpu.make_async_remote_copy(
                self.view(at), self.view(at), self.ss[n], self.rs[n],
                device_id={self.axis: to}, device_id_type=MESH,
            )

        def start(self):
            self.copy(self.me, 0, self.ahead).start()
            self.copy(self.me, 1, self.behind).start()

        def forward(self):
            wait(self.view(self.behind), self.rs[0])
            self.copy(self.behind, 2, self.ahead).start()

        def finish(self):
            wait(self.view(self.ahead), self.rs[1])
            wait(self.view(self.opposite), self.rs[2])

        def sent(self):
            wait(self.view(self.me), self.ss[0])
            wait(self.view(self.me), self.ss[1])
            wait(self.view(self.behind), self.ss[2])

    class Direct(Gather):
        def start(self):
            for n, to in enumerate((self.ahead, self.behind, self.opposite)):
                self.copy(self.me, n, to).start()

        def take(self, n):
            wait(self.view((self.behind, self.ahead, self.opposite)[n]), self.rs[n])

        def sent(self):
            for n in range(3):
                wait(self.view(self.me), self.ss[n])

    xends, yends = (xa, xb, xo), (ya, yb, yo)
    first = [
        (Direct(lambda n, h=h: gx[h].at[n, y], x, "dp", xends, h, 0, 4),
         Direct(lambda n, h=h: gc[h].at[x, n], y, "helper", yends, h, 1, 4))
        for h in range(parts)
    ]
    xroles, yroles = (x, xb, xa, xo), (y, yb, ya, yo)
    second = [
        [(Gather(lambda n, h=h, k=k: gx[h].at[xroles[k], n], y, "helper", yends, h, 0, k),
          Gather(lambda n, h=h, k=k: gc[h].at[n, yroles[k]], x, "dp", xends, h, 1, k))
         for k in range(4)]
        for h in range(parts)
    ]

    def arrive(h):
        wait(rb[h], zr.at[h])
        width = cuts[h]
        for s in range(8):
            rows = rb[h][s].astype(F32)
            stage[2 * s : 2 * s + 2, 0:width] = rows[0:2]
            stage[16 + 2 * s : 18 + 2 * s, 0:width] = rows[2:4]
        gx[h][x, y] = stage[0:16, 0:width].astype(BF16)
        gc[h][x, y] = stage[16:32, 0:width].astype(BF16)
        run(first[h], "start")
        run(second[h][0], "start")

    def run(group, what, *args):
        for g in group:
            getattr(g, what)(*args)

    def pass_on(h):
        for group in second[h]:
            run(group, "forward")

    for h in range(parts):
        arrive(h)
        for n in range(3):
            run(first[h], "take", n)
            run(second[h][n + 1], "start")
        if 0 < h < parts - 1:
            pass_on(h - 1)

    total = 256
    pre = jnp.zeros((total, 256), F32)
    d_hidden = jnp.zeros((total, 128), F32)
    for load in loads:
        load.wait()
    for h in range(parts):
        if h >= max(parts - 2, 0) or parts == 1:
            pass_on(h)
        for group in second[h]:
            run(group, "finish")
        width = cuts[h]
        start = sum(cuts[:h])
        pre = pre + dot(gx[h][...].reshape(total, width), wcat[start : start + width, :])
        d_hidden = d_hidden + dot(gc[h][...].reshape(total, width), wd[start : start + width, :])

    gate_pre = pre[:, 0:128]
    up1 = pre[:, 128:256] + 1.0
    sig = jax.nn.sigmoid(1.702 * gate_pre)
    activated = gate_pre * sig
    hidden = (up1 * activated).astype(BF16)
    d_up = (d_hidden * activated).astype(BF16)
    d_gate = (d_hidden * up1 * (sig + 1.702 * gate_pre * sig * (1.0 - sig))).astype(BF16)
    dcat = jnp.concatenate([d_gate, d_up], axis=1)

    for q in range(4):
        part = dot(dcat, wcat[quarter * q : quarter * (q + 1), :], NT)
        for n in range(4):
            for k in range(2):
                at = 64 * n + 16 * k
                pu[k, n, q] = part[at : at + 16, :].astype(BF16)
                pv[k, n, q] = part[at + 32 : at + 48, :].astype(BF16)

    class Scatter:
        def __init__(self, view, land, me, axis, ends, k, a, phase):
            self.view, self.land, self.me, self.axis = view, land, me, axis
            self.ahead, self.behind, self.opposite = ends
            self.ss = [rss.at[k, a, phase, n] for n in range(3)]
            self.rs = [rsr.at[k, a, phase, n] for n in range(3)]

        def copy(self, at, n, to):
            return pltpu.make_async_remote_copy(
                self.view(at), self.land.at[n], self.ss[n], self.rs[n],
                device_id={self.axis: to}, device_id_type=MESH,
            )

        def start(self):
            self.copy(self.opposite, 0, self.ahead).start()
            self.copy(self.behind, 1, self.behind).start()

        def forward(self):
            wait(self.land.at[0], self.rs[0])
            ref = self.view(self.ahead)
            ref[...] = (ref[...].astype(F32) + self.land[0].astype(F32)).astype(BF16)
            self.copy(self.ahead, 2, self.ahead).start()

        def finish(self):
            wait(self.land.at[1], self.rs[1])
            wait(self.land.at[2], self.rs[2])
            return self.view(self.me)[...].astype(F32) + self.land[1].astype(F32) + self.land[2].astype(F32)

        def sent(self):
            for n in range(3):
                wait(self.land.at[n], self.ss[n])

    class DirectScatter(Scatter):
        def start(self):
            for n, to in enumerate((self.ahead, self.behind, self.opposite)):
                self.copy(to, n, to).start()

        def finish(self):
            for n in range(3):
                wait(self.land.at[n], self.rs[n])
            terms = [self.land[n].astype(F32) for n in range(3)]
            return self.view(self.me)[...].astype(F32) + terms[0] + terms[1] + terms[2]

    one = [
        (Scatter(lambda n, k=k: pu.at[k, n], ru.at[k], x, "dp", xends, k, 0, 0),
         Scatter(lambda n, k=k: pv.at[k, :, n], rv.at[k], y, "helper", yends, k, 1, 0))
        for k in range(2)
    ]
    two = [
        (DirectScatter(lambda n, k=k: qu.at[k, n], su.at[k], y, "helper", yends, k, 0, 1),
         DirectScatter(lambda n, k=k: qv.at[k, n], sv.at[k], x, "dp", xends, k, 1, 1))
        for k in range(2)
    ]
    for k in range(2):
        run(one[k], "start")

    def weight_grads(h, begin, end):
        cut = slice(begin, end)
        both = dot(gx[h][:, :, :, cut].reshape(total, end - begin), dcat, TN).astype(BF16)
        gg[cut, :] = both[:, 0:128]
        gu[cut, :] = both[:, 128:256]
        gd[cut, :] = dot(gc[h][:, :, :, cut].reshape(total, end - begin), hidden, TN).astype(BF16)

    def give_back(plane, rows):
        back[16 * plane : 16 * plane + 16, :] = rows
        for i in (2, 3, 0, 1):
            to = (z - shift(i, plane) + nz) % nz
            for core in range(2):
                base = (plane * 4 + i) * 2
                m = base + core
                ts[m] = back[2 * m : 2 * m + 2, :].astype(BF16)
                far = pltpu.make_async_remote_copy(
                    ts.at[m], tr.at[base + c], ts_sem, tr_sem,
                    device_id={"expert": to * 2 + core}, device_id_type=MESH,
                )
                if shift(i, plane) == 0:

                    @pl.when(c == core)
                    def _():
                        pltpu.make_async_copy(ts.at[m], tr.at[base + c], tr_sem).start()

                    @pl.when(c != core)
                    def _():
                        far.start()
                else:
                    far.start()

    run(one[0], "forward")
    run(one[1], "forward")
    for k in range(2):
        qu[k] = one[k][0].finish().astype(BF16)
        two[k][0].start()
        qv[k] = one[k][1].finish().astype(BF16)
        two[k][1].start()
    for k in range(2):
        give_back(k, two[k][0].finish())
        give_back(2 + k, two[k][1].finish())
    weight_grads(0, 0, model)
    r = lax.broadcasted_iota(jnp.int32, (64, 1), 0)
    home, _ = pick(idt, gvt, z, nz, (r // 4) % 4, r // 16, (r // 2) % 2, r % 2)
    wait(tr, tr_sem)
    for m in range(32):
        back[2 * m : 2 * m + 2, :] = tr[m].astype(F32)
    gi_ref[...] = dot(home.astype(BF16), back[...].astype(BF16), TN).astype(BF16)

    for h in range(parts):
        @pl.when(y == 0)
        def _():
            wait(sb[h].at[0:7], zs.at[h])

        @pl.when(y != 0)
        def _():
            wait(sb[h], zs.at[h])

        run(first[h], "sent")
        for group in second[h]:
            run(group, "sent")
    for k in range(2):
        run(one[k], "sent")
        run(two[k], "sent")
    wait(ts.at[0:31], ts_sem)


def hand_over(*refs):
    copies = [pltpu.make_async_copy(refs[n], refs[4 + n], refs[8].at[n]) for n in range(4)]
    for copy in copies:
        copy.start()
    for copy in copies:
        copy.wait()


def local(inputs, cotangent, expert_ids, gate_values, w_gate, w_up, w_down):
    tokens, model = inputs.shape
    nz = lax.axis_size("expert") // 2
    hidden = w_gate.shape[2]
    quarter = model // 4
    cuts = (model,)
    vmem = pl.BlockSpec(memory_space=pltpu.VMEM)
    anywhere = pl.BlockSpec(memory_space=pl.ANY)
    scratch = [pltpu.VMEM((8, 4, w), BF16) for w in cuts]
    scratch += [pltpu.VMEM((8, 4, w), BF16) for w in cuts]
    scratch += [pltpu.VMEM((4, 4, 16, w), BF16) for w in cuts]
    scratch += [pltpu.VMEM((4, 4, 16, w), BF16) for w in cuts]
    scratch += [
        pltpu.VMEM((tokens, model), BF16),
        pltpu.VMEM((tokens, model), BF16),
        pltpu.VMEM(expert_ids.shape[::-1], expert_ids.dtype),
        pltpu.VMEM(gate_values.shape[::-1], gate_values.dtype),
        pltpu.VMEM((model, 2 * hidden), BF16),
        pltpu.VMEM((model, hidden), BF16),
        pltpu.VMEM((32, max(cuts)), F32),
        pltpu.VMEM((2, 4, 4, 16, quarter), BF16),
        pltpu.VMEM((2, 4, 4, 16, quarter), BF16),
        pltpu.VMEM((2, 3, 4, 16, quarter), BF16),
        pltpu.VMEM((2, 3, 4, 16, quarter), BF16),
        pltpu.VMEM((2, 4, 16, quarter), BF16),
        pltpu.VMEM((2, 4, 16, quarter), BF16),
        pltpu.VMEM((2, 3, 16, quarter), BF16),
        pltpu.VMEM((2, 3, 16, quarter), BF16),
        pltpu.VMEM((64, quarter), F32),
        pltpu.VMEM((32, 2, quarter), BF16),
        pltpu.VMEM((32, 2, quarter), BF16),
        pltpu.SemaphoreType.DMA((len(cuts),)),
        pltpu.SemaphoreType.DMA((len(cuts),)),
        pltpu.SemaphoreType.DMA((len(cuts), 2, 5, 3)),
        pltpu.SemaphoreType.DMA((len(cuts), 2, 5, 3)),
        pltpu.SemaphoreType.DMA((2, 2, 2, 3)),
        pltpu.SemaphoreType.DMA((2, 2, 2, 3)),
        pltpu.SemaphoreType.DMA,
        pltpu.SemaphoreType.DMA,
        pltpu.SemaphoreType.DMA((4,)),
        pltpu.SemaphoreType.DMA((3,)),
    ]
    grad = pltpu.VMEM((model, hidden), BF16)
    grads = pl.pallas_call(
        functools.partial(body, cuts, nz),
        out_shape=(pltpu.VMEM((tokens, quarter), BF16), grad, grad, grad),
        in_specs=[anywhere] * 7,
        out_specs=(vmem,) * 4,
        scratch_shapes=scratch,
        compiler_params=pltpu.CompilerParams(
            collective_id=0, has_side_effects=True, vmem_limit_bytes=56 * 1024 * 1024
        ),
    )(
        inputs,
        cotangent,
        expert_ids.T,
        gate_values.T,
        w_gate[0],
        w_up[0],
        w_down[0].T,
    )
    gi, gg, gu, gd = pl.pallas_call(
        hand_over,
        out_shape=tuple(jax.ShapeDtypeStruct(g.shape, g.dtype) for g in grads),
        in_specs=[anywhere] * 4,
        out_specs=(anywhere,) * 4,
        scratch_shapes=[pltpu.SemaphoreType.DMA((4,))],
    )(*(pltpu.with_memory_space_constraint(g, pltpu.VMEM) for g in grads))
    return gi, gg[None], gu[None], gd.T[None]


def solution(mesh):
    in_specs = (
        P(("expert", "dp"), None),
        P(("expert", "dp"), None),
        P(("expert", "dp"), None),
        P(("expert", "dp"), None),
        P("expert", None, ("helper", "dp")),
        P("expert", None, ("helper", "dp")),
        P("expert", ("helper", "dp"), None),
    )
    out_specs = (
        P(("expert", "dp"), "helper"),
        P("expert", None, ("helper", "dp")),
        P("expert", None, ("helper", "dp")),
        P("expert", ("helper", "dp"), None),
    )
    return jax.shard_map(local, mesh=mesh, in_specs=in_specs, out_specs=out_specs, check_vma=False)
```

```python
import functools

import jax
import jax.numpy as jnp
from jax import lax
from jax.experimental import pallas as pl
from jax.experimental.pallas import tpu as pltpu
from jax.sharding import PartitionSpec as P

CAP = 2
MESH = pl.DeviceIdType.MESH
F32 = jnp.float32
BF16 = jnp.bfloat16
NT = (((1,), (1,)), ((), ()))
TN = (((0,), (0,)), ((), ()))
NN = (((1,), (0,)), ((), ()))


def dot(a, b, dims=NN):
    return lax.dot_general(a, b, dims, preferred_element_type=F32)


def shift(i, y):
    none = 1 - (y + 3) // 4
    return (y + 4 * none, -y - 4 * none, 8 - y, (y - 8) * (1 - none))[i]


def pick_shift(i, y):
    a, b, c, d = (shift(n, y) for n in range(4))
    return jnp.where(i == 0, a, jnp.where(i == 1, b, jnp.where(i == 2, c, d)))


def pick(idt, gvt, z, nz, i, y, core, j):
    far = z + pick_shift(i, y)
    far = jnp.where(far < 0, far + nz, jnp.where(far >= nz, far - nz, far))
    expert = far * 2 + core
    tokens = idt.shape[1]
    hits = [(idt[k : k + 1, :] == expert) for k in range(idt.shape[0])]
    named = functools.reduce(lambda a, b: a + b, [h.astype(F32) for h in hits])
    row = lax.broadcasted_iota(jnp.int32, (tokens, tokens), 0)
    col = lax.broadcasted_iota(jnp.int32, (tokens, tokens), 1)
    before = dot(named.astype(BF16), (row < col).astype(BF16))
    chosen = jnp.where(before == j.astype(F32), named, 0.0)
    weight = functools.reduce(lambda a, b: a + b, [h.astype(F32) * gvt[k : k + 1, :] for k, h in enumerate(hits)])
    return chosen, jnp.sum(chosen * weight, axis=1, keepdims=True)


def body(cuts, nz, x_hbm, c_hbm, idt_hbm, gvt_hbm, wg_hbm, wu_hbm, wd_hbm, gi_ref, gg, gu, gd, *rest):
    parts = len(cuts)
    sb, rb, gx, gc = (rest[n * parts : (n + 1) * parts] for n in range(4))
    (x_ref, c_ref, idt_ref, gvt_ref, wcat, wd, stage, pu, pv, ru, rv, qu, qv, su, sv, back, ts, tr,
     zs, zr, ags, agr, rss, rsr, ts_sem, tr_sem, isem, wsem) = rest[4 * parts :]
    e = lax.axis_index("expert")
    y = lax.axis_index("helper")
    x = lax.axis_index("dp")
    ne = 2 * nz
    z = e // 2
    c = e % 2
    model = x_hbm.shape[1]
    quarter = model // 4

    def ring(me):
        return (me + 1 + 2 * c) % 4, (me + 3 - 2 * c) % 4, (me + 2) % 4

    xa, xb, xo = ring(x)
    ya, yb, yo = ring(y)

    barrier = pltpu.get_barrier_semaphore()

    for n in sorted(range(1, ne), key=lambda n: -min(n, ne - n)):
        pl.semaphore_signal(barrier, inc=1, device_id={"expert": (e + n) % ne}, device_id_type=MESH)

    for other in (xa, xb, xo):
        pl.semaphore_signal(barrier, inc=1, device_id={"dp": other}, device_id_type=MESH)
    for other in (ya, yb, yo):
        pl.semaphore_signal(barrier, inc=1, device_id={"helper": other}, device_id_type=MESH)

    fetches = [
        pltpu.make_async_copy(idt_hbm, idt_ref, isem.at[0]),
        pltpu.make_async_copy(gvt_hbm, gvt_ref, isem.at[1]),
        pltpu.make_async_copy(x_hbm, x_ref, isem.at[2]),
        pltpu.make_async_copy(c_hbm, c_ref, isem.at[3]),
    ]
    for fetch in fetches:
        fetch.start()
    loads = [
        pltpu.make_async_copy(wg_hbm, wcat.at[:, 0:128], wsem.at[0]),
        pltpu.make_async_copy(wu_hbm, wcat.at[:, 128:256], wsem.at[1]),
        pltpu.make_async_copy(wd_hbm, wd, wsem.at[2]),
    ]
    for load in loads:
        load.start()
    for fetch in fetches:
        fetch.wait()

    idt = idt_ref[...]
    gvt = gvt_ref[...]
    r = lax.broadcasted_iota(jnp.int32, (32, 1), 0)
    half = (r // 2) % 2
    chosen, gate = pick(idt, gvt, z, nz, r // 8, y, (r // 4) % 2, r % 2)
    pick_x = jnp.where(half == 0, chosen, 0.0).astype(BF16)
    pick_c = jnp.where(half == 1, chosen, 0.0).astype(BF16)
    start = 0
    for h, width in enumerate(cuts):
        rows = dot(pick_x, x_ref[:, start : start + width]) + gate * dot(pick_c, c_ref[:, start : start + width])
        for s in range(8):
            sb[h][s] = rows[4 * s : 4 * s + 4, :].astype(BF16)
        start += width

    pl.semaphore_wait(barrier, ne - 1 + 6)

    def wait(ref, sem):
        pltpu.make_async_copy(ref, ref, sem).wait()

    for h in range(parts):
        for i in (2, 3, 0, 1):
            to = (z + shift(i, y) + nz) % nz
            for core in range(2):
                s = 2 * i + core
                far = pltpu.make_async_remote_copy(
                    sb[h].at[s], rb[h].at[2 * i + c], zs.at[h], zr.at[h],
                    device_id={"expert": to * 2 + core}, device_id_type=MESH,
                )
                if i == 3:
                    own = (y == 0) & (c == core)

                    @pl.when(own)
                    def _():
                        pltpu.make_async_copy(sb[h].at[s], rb[h].at[2 * i + c], zr.at[h]).start()

                    @pl.when(jnp.logical_not(own))
                    def _():
                        far.start()
                else:
                    far.start()

    class Gather:
        def __init__(self, view, me, axis, ends, h, a, phase):
            self.view, self.me, self.axis = view, me, axis
            self.ahead, self.behind, self.opposite = ends
            self.ss = [ags.at[h, a, phase, n] for n in range(3)]
            self.rs = [agr.at[h, a, phase, n] for n in range(3)]

        def copy(self, at, n, to):
            return pltpu.make_async_remote_copy(
                self.view(at), self.view(at), self.ss[n], self.rs[n],
                device_id={self.axis: to}, device_id_type=MESH,
            )

        def start(self):
            self.copy(self.me, 0, self.ahead).start()
            self.copy(self.me, 1, self.behind).start()

        def forward(self):
            wait(self.view(self.behind), self.rs[0])
            self.copy(self.behind, 2, self.ahead).start()

        def take(self, n):
            if n == 0:
                self.forward()
            else:
                wait(self.view((self.ahead, self.opposite)[n - 1]), self.rs[n])

        def finish(self):
            self.take(1)
            self.take(2)

        def sent(self):
            wait(self.view(self.me), self.ss[0])
            wait(self.view(self.me), self.ss[1])
            wait(self.view(self.behind), self.ss[2])

    xends, yends = (xa, xb, xo), (ya, yb, yo)
    first = [
        (Gather(lambda n, h=h: gx[h].at[n, y], x, "dp", xends, h, 0, 4),
         Gather(lambda n, h=h: gc[h].at[x, n], y, "helper", yends, h, 1, 4))
        for h in range(parts)
    ]
    xroles, yroles = (x, xb, xa, xo), (y, yb, ya, yo)
    second = [
        [(Gather(lambda n, h=h, k=k: gx[h].at[xroles[k], n], y, "helper", yends, h, 0, k),
          Gather(lambda n, h=h, k=k: gc[h].at[n, yroles[k]], x, "dp", xends, h, 1, k))
         for k in range(4)]
        for h in range(parts)
    ]

    def arrive(h):
        wait(rb[h], zr.at[h])
        width = cuts[h]
        for a, there in enumerate((gx, gc)):
            for s in range(8):
                stage[2 * s : 2 * s + 2, 0:width] = rb[h][s].astype(F32)[2 * a : 2 * a + 2]
            there[h][x, y] = stage[0:16, 0:width].astype(BF16)
            first[h][a].start()
        run(second[h][0], "start")

    def run(group, what, *args):
        for g in group:
            getattr(g, what)(*args)

    def pass_on(h):
        for group in second[h]:
            run(group, "forward")

    for h in range(parts):
        arrive(h)
        for n in range(3):
            run(first[h], "take", n)
            run(second[h][n + 1], "start")
        if 0 < h < parts - 1:
            pass_on(h - 1)

    total = 256
    pre = jnp.zeros((total, 256), F32)
    d_hidden = jnp.zeros((total, 128), F32)
    for load in loads:
        load.wait()
    for h in range(parts):
        if h >= max(parts - 2, 0) or parts == 1:
            pass_on(h)
        for group in second[h]:
            run(group, "finish")
        width = cuts[h]
        start = sum(cuts[:h])
        pre = pre + dot(gx[h][...].reshape(total, width), wcat[start : start + width, :])
        d_hidden = d_hidden + dot(gc[h][...].reshape(total, width), wd[start : start + width, :])

    gate_pre = pre[:, 0:128]
    up1 = pre[:, 128:256] + 1.0
    sig = jax.nn.sigmoid(1.702 * gate_pre)
    activated = gate_pre * sig
    hidden = (up1 * activated).astype(BF16)
    d_up = (d_hidden * activated).astype(BF16)
    d_gate = (d_hidden * up1 * (sig + 1.702 * gate_pre * sig * (1.0 - sig))).astype(BF16)
    dcat = jnp.concatenate([d_gate, d_up], axis=1)

    for q in range(4):
        part = dot(dcat, wcat[quarter * q : quarter * (q + 1), :], NT)
        for n in range(4):
            for k in range(2):
                at = 64 * n + 16 * k
                pu[k, n, q] = part[at : at + 16, :].astype(BF16)
                pv[k, n, q] = part[at + 32 : at + 48, :].astype(BF16)

    class Scatter:
        def __init__(self, view, land, me, axis, ends, k, a, phase):
            self.view, self.land, self.me, self.axis = view, land, me, axis
            self.ahead, self.behind, self.opposite = ends
            self.ss = [rss.at[k, a, phase, n] for n in range(3)]
            self.rs = [rsr.at[k, a, phase, n] for n in range(3)]

        def copy(self, at, n, to):
            return pltpu.make_async_remote_copy(
                self.view(at), self.land.at[n], self.ss[n], self.rs[n],
                device_id={self.axis: to}, device_id_type=MESH,
            )

        def start(self):
            self.copy(self.opposite, 0, self.ahead).start()

        def start_last(self):
            self.copy(self.behind, 1, self.behind).start()

        def forward(self):
            wait(self.land.at[0], self.rs[0])
            ref = self.view(self.ahead)
            ref[...] = (ref[...].astype(F32) + self.land[0].astype(F32)).astype(BF16)
            self.copy(self.ahead, 2, self.ahead).start()

        def finish(self):
            wait(self.land.at[1], self.rs[1])
            wait(self.land.at[2], self.rs[2])
            return self.view(self.me)[...].astype(F32) + self.land[1].astype(F32) + self.land[2].astype(F32)

        def sent(self):
            for n in range(3):
                wait(self.land.at[n], self.ss[n])

    class DirectScatter(Scatter):
        def start(self):
            for n, to in ((2, self.opposite), (0, self.ahead), (1, self.behind)):
                self.copy(to, n, to).start()

        def finish(self):
            for n in range(3):
                wait(self.land.at[n], self.rs[n])
            terms = [self.land[n].astype(F32) for n in range(3)]
            return self.view(self.me)[...].astype(F32) + terms[0] + terms[1] + terms[2]

    one = [
        (Scatter(lambda n, k=k: pu.at[k, n], ru.at[k], x, "dp", xends, k, 0, 0),
         Scatter(lambda n, k=k: pv.at[k, :, n], rv.at[k], y, "helper", yends, k, 1, 0))
        for k in range(2)
    ]
    two = [
        (DirectScatter(lambda n, k=k: qu.at[k, n], su.at[k], y, "helper", yends, k, 0, 1),
         DirectScatter(lambda n, k=k: qv.at[k, n], sv.at[k], x, "dp", xends, k, 1, 1))
        for k in range(2)
    ]
    for k in range(2):
        run(one[k], "start")
    for k in range(2):
        run(one[k], "start_last")

    def weight_grads(h, begin, end):
        cut = slice(begin, end)
        both = dot(gx[h][:, :, :, cut].reshape(total, end - begin), dcat, TN).astype(BF16)
        gg[cut, :] = both[:, 0:128]
        gu[cut, :] = both[:, 128:256]
        gd[cut, :] = dot(gc[h][:, :, :, cut].reshape(total, end - begin), hidden, TN).astype(BF16)

    def give_back(plane, rows):
        back[16 * plane : 16 * plane + 16, :] = rows
        for i in (2, 3, 0, 1):
            to = (z - shift(i, plane) + nz) % nz
            for core in range(2):
                base = (plane * 4 + i) * 2
                m = base + core
                ts[m] = back[2 * m : 2 * m + 2, :].astype(BF16)
                far = pltpu.make_async_remote_copy(
                    ts.at[m], tr.at[base + c], ts_sem, tr_sem,
                    device_id={"expert": to * 2 + core}, device_id_type=MESH,
                )
                if shift(i, plane) == 0:

                    @pl.when(c == core)
                    def _():
                        pltpu.make_async_copy(ts.at[m], tr.at[base + c], tr_sem).start()

                    @pl.when(c != core)
                    def _():
                        far.start()
                else:
                    far.start()

    run(one[0], "forward")
    run(one[1], "forward")
    for k in range(2):
        qu[k] = one[k][0].finish().astype(BF16)
        two[k][0].start()
        qv[k] = one[k][1].finish().astype(BF16)
        two[k][1].start()
    for k in range(2):
        give_back(k, two[k][0].finish())
        give_back(2 + k, two[k][1].finish())
    weight_grads(0, 0, model)
    r = lax.broadcasted_iota(jnp.int32, (64, 1), 0)
    home, _ = pick(idt, gvt, z, nz, (r // 4) % 4, r // 16, (r // 2) % 2, r % 2)
    wait(tr, tr_sem)
    for m in range(32):
        back[2 * m : 2 * m + 2, :] = tr[m].astype(F32)
    gi_ref[...] = dot(home.astype(BF16), back[...].astype(BF16), TN).astype(BF16)

    for h in range(parts):
        @pl.when(y == 0)
        def _():
            wait(sb[h].at[0:7], zs.at[h])

        @pl.when(y != 0)
        def _():
            wait(sb[h], zs.at[h])

        run(first[h], "sent")
        for group in second[h]:
            run(group, "sent")
    for k in range(2):
        run(one[k], "sent")
        run(two[k], "sent")
    wait(ts.at[0:31], ts_sem)


def hand_over(*refs):
    copies = [pltpu.make_async_copy(refs[n], refs[4 + n], refs[8].at[n]) for n in range(4)]
    for copy in copies:
        copy.start()
    for copy in copies:
        copy.wait()


def local(inputs, cotangent, expert_ids, gate_values, w_gate, w_up, w_down):
    tokens, model = inputs.shape
    nz = lax.axis_size("expert") // 2
    hidden = w_gate.shape[2]
    quarter = model // 4
    cuts = (model,)
    vmem = pl.BlockSpec(memory_space=pltpu.VMEM)
    anywhere = pl.BlockSpec(memory_space=pl.ANY)
    scratch = [pltpu.VMEM((8, 4, w), BF16) for w in cuts]
    scratch += [pltpu.VMEM((8, 4, w), BF16) for w in cuts]
    scratch += [pltpu.VMEM((4, 4, 16, w), BF16) for w in cuts]
    scratch += [pltpu.VMEM((4, 4, 16, w), BF16) for w in cuts]
    scratch += [
        pltpu.VMEM((tokens, model), BF16),
        pltpu.VMEM((tokens, model), BF16),
        pltpu.VMEM(expert_ids.shape[::-1], expert_ids.dtype),
        pltpu.VMEM(gate_values.shape[::-1], gate_values.dtype),
        pltpu.VMEM((model, 2 * hidden), BF16),
        pltpu.VMEM((model, hidden), BF16),
        pltpu.VMEM((32, max(cuts)), F32),
        pltpu.VMEM((2, 4, 4, 16, quarter), BF16),
        pltpu.VMEM((2, 4, 4, 16, quarter), BF16),
        pltpu.VMEM((2, 3, 4, 16, quarter), BF16),
        pltpu.VMEM((2, 3, 4, 16, quarter), BF16),
        pltpu.VMEM((2, 4, 16, quarter), BF16),
        pltpu.VMEM((2, 4, 16, quarter), BF16),
        pltpu.VMEM((2, 3, 16, quarter), BF16),
        pltpu.VMEM((2, 3, 16, quarter), BF16),
        pltpu.VMEM((64, quarter), F32),
        pltpu.VMEM((32, 2, quarter), BF16),
        pltpu.VMEM((32, 2, quarter), BF16),
        pltpu.SemaphoreType.DMA((len(cuts),)),
        pltpu.SemaphoreType.DMA((len(cuts),)),
        pltpu.SemaphoreType.DMA((len(cuts), 2, 5, 3)),
        pltpu.SemaphoreType.DMA((len(cuts), 2, 5, 3)),
        pltpu.SemaphoreType.DMA((2, 2, 2, 3)),
        pltpu.SemaphoreType.DMA((2, 2, 2, 3)),
        pltpu.SemaphoreType.DMA,
        pltpu.SemaphoreType.DMA,
        pltpu.SemaphoreType.DMA((4,)),
        pltpu.SemaphoreType.DMA((3,)),
    ]
    grad = pltpu.VMEM((model, hidden), BF16)
    grads = pl.pallas_call(
        functools.partial(body, cuts, nz),
        out_shape=(pltpu.VMEM((tokens, quarter), BF16), grad, grad, grad),
        in_specs=[anywhere] * 7,
        out_specs=(vmem,) * 4,
        scratch_shapes=scratch,
        compiler_params=pltpu.CompilerParams(
            collective_id=0, has_side_effects=True, vmem_limit_bytes=56 * 1024 * 1024
        ),
    )(
        inputs,
        cotangent,
        expert_ids.T,
        gate_values.T,
        w_gate[0],
        w_up[0],
        w_down[0].T,
    )
    gi, gg, gu, gd = pl.pallas_call(
        hand_over,
        out_shape=tuple(jax.ShapeDtypeStruct(g.shape, g.dtype) for g in grads),
        in_specs=[anywhere] * 4,
        out_specs=(anywhere,) * 4,
        scratch_shapes=[pltpu.SemaphoreType.DMA((4,))],
    )(*(pltpu.with_memory_space_constraint(g, pltpu.VMEM) for g in grads))
    return gi, gg[None], gu[None], gd.T[None]


def solution(mesh):
    in_specs = (
        P(("expert", "dp"), None),
        P(("expert", "dp"), None),
        P(("expert", "dp"), None),
        P(("expert", "dp"), None),
        P("expert", None, ("helper", "dp")),
        P("expert", None, ("helper", "dp")),
        P("expert", ("helper", "dp"), None),
    )
    out_specs = (
        P(("expert", "dp"), "helper"),
        P("expert", None, ("helper", "dp")),
        P("expert", None, ("helper", "dp")),
        P("expert", ("helper", "dp"), None),
    )
    return jax.shard_map(local, mesh=mesh, in_specs=in_specs, out_specs=out_specs, check_vma=False)
```
